32 devices in a mesh: shard: 4 (over y, x), rep: 8 (over z, core).
Axes of the slice: x: 2, y: 2, z: 4, core: 2. Of those that a mesh axis runs over, the one named last changes fastest.
Arguments:
- latents: bfloat16 [96, 256, 384], P(('shard', 'rep')), may hold values from -6 to 6
- cotangent: bfloat16 [96, 256, 384], P(('shard', 'rep')), may hold values from -6 to 6
- timesteps: int32 [96], P(('shard', 'rep')), may hold values from 0 to 999
- labels: int32 [96], P(('shard', 'rep')), may hold values from 0 to 1000
- time_table: float32 [1000, 384], replicated, may hold values from -6 to 6
- class_table: float32 [1001, 384], replicated, may hold values from -6 to 6
- w_ada: bfloat16 [384, 2304], P('shard'), may hold values from -0.3125 to 0.3125
- b_ada: bfloat16 [2304], P('shard'), may hold values from -3 to 3
- w_qkv: bfloat16 [384, 1152], P('shard'), may hold values from -1.5 to 1.5, as said below
- b_qv: bfloat16 [768], P('shard'), may hold values from -3 to 3
- w_out: bfloat16 [384, 384], P('shard'), may hold values from -1.25 to 1.25
- b_out: bfloat16 [384], P('shard'), may hold values from -6 to 6
- w_up: bfloat16 [384, 1536], P('shard'), may hold values from -0.3125 to 0.3125
- b_up: bfloat16 [1536], P('shard'), may hold values from -3 to 3
- w_down: bfloat16 [1536, 384], P('shard'), may hold values from -0.15625 to 0.15625
- b_down: bfloat16 [384], P('shard'), may hold values from -6 to 6
Outputs:
- block_out: float32 [96, 256, 384], P(('shard', 'rep'))
- input_grad: float32 [96, 256, 384], P(('shard', 'rep'))
- cond_grad: float32 [96, 384], P(('shard', 'rep'))
- grad_w_ada: float32 [384, 2304], P('shard')
- grad_b_ada: float32 [2304], P('shard')
- grad_w_qkv: float32 [384, 1152], P('shard')
- grad_b_qv: float32 [768], P('shard')
- grad_w_out: float32 [384, 384], P('shard')
- grad_b_out: float32 [384], P('shard')
- grad_w_up: float32 [384, 1536], P('shard')
- grad_b_up: float32 [1536], P('shard')
- grad_w_down: float32 [1536, 384], P('shard')
- grad_b_down: float32 [384], P('shard')
The draws below stay inside these ranges and needn't reach their ends.
Inputs may be any that keep to these rules, and one draw needn't show every extreme that they name: `w_qkv`: entries of the projections are independent.
All inputs are finite; a program needn't handle non-finite values.
Results may differ from the reference program's by a relative error of at most 0.011.
The reference program's roundings to bfloat16 on the way count: a program that leaves them out, or rounds other values in their place, can miss the bound.
Values may be sent and summed in bfloat16 or wider, within the bound.
A program may use at most 128 MiB of HBM per device.

```python
import math
import jax
import jax.numpy as jnp
from jax import lax

D = 384
H = 6
HD = 64
FF = 1536
S = 256
STEPS = 1000
CLASSES = 1001
SEQS = 96


def draw_w_qkv(key, part):
    key_all = jax.random.fold_in(key, 11)
    joined = jax.random.normal(key_all, (D, 3 * D), jnp.float32) / math.sqrt(D)
    return jnp.clip(joined, -1.5, 1.5).astype(jnp.bfloat16)


def touch_ends(values, key, low, high):
    longest = values.shape.index(max(values.shape))
    spots = []
    for shift in (0, 1):
        where = [jax.random.randint(jax.random.fold_in(key, axis), (), 0, length) for axis, length in enumerate(values.shape)]
        where[longest] = (where[longest] + shift) % values.shape[longest]
        spots.append(tuple(where))
    return values.at[spots[0]].set(low).at[spots[1]].set(high)


def shard_levels(stream_key, dims, shards, least, largest):
    def one(position, parts):
        heights = jax.random.uniform(jax.random.fold_in(jax.random.fold_in(stream_key, 6), position), (parts,), jnp.float32, least / len(shards), largest / len(shards))
        return jnp.repeat(jnp.exp(heights), dims[position] // parts).reshape((-1,) + (1,) * (len(dims) - position - 1))

    level = one(*shards[0])
    for cut in shards[1:]:
        level = level * one(*cut)
    return level


def scatter_about(key, shape, scale, bound, pieces=(), held_as=jnp.bfloat16):
    factor_of = shard_levels(key, shape, pieces, -0.22, 0.18) if pieces else 1.0
    result = jax.random.normal(key, shape, jnp.float32) * scale * factor_of
    return jnp.minimum(jnp.maximum(result, -bound), bound).astype(held_as)


def setup_inputs(seed: int = 0) -> dict:
    splits = jax.random.split(jax.random.key(seed), 17)
    return {
        "latents": scatter_about(splits[0], (SEQS, S, D), 1.0, 6.0, ((0, 32),)),
        "cotangent": scatter_about(splits[1], (SEQS, S, D), 1.0, 6.0, ((0, 32),)),
        "timesteps": touch_ends(jax.random.randint(splits[2], (SEQS,), 0, STEPS), jax.random.fold_in(splits[2], 1), 0, STEPS - 1).astype(jnp.int32),
        "labels": touch_ends(jax.random.randint(splits[3], (SEQS,), 0, CLASSES), jax.random.fold_in(splits[3], 1), 0, CLASSES - 1).astype(jnp.int32),
        "time_table": scatter_about(splits[4], (STEPS, D), 1.0, 6.0, (), jnp.float32),
        "class_table": scatter_about(splits[5], (CLASSES, D), 1.0, 6.0, (), jnp.float32),
        "w_ada": scatter_about(splits[6], (D, 6 * D), D ** -0.5, 0.3125, ((0, 4),)),
        "b_ada": scatter_about(splits[7], (6 * D,), 0.5, 3.0, ((0, 4),)),
        "w_qkv": draw_w_qkv(jax.random.fold_in(splits[16], 71), 0),
        "b_qv": scatter_about(splits[9], (2 * D,), 0.5, 3.0, ((0, 4),)),
        "w_out": scatter_about(splits[10], (D, D), (D // 16) ** -0.5, 1.25, ((0, 4),)),
        "b_out": scatter_about(splits[11], (D,), 1.0, 6.0, ((0, 4),)),
        "w_up": scatter_about(splits[12], (D, FF), D ** -0.5, 0.3125, ((0, 4),)),
        "b_up": scatter_about(splits[13], (FF,), 0.5, 3.0, ((0, 4),)),
        "w_down": scatter_about(splits[14], (FF, D), FF ** -0.5, 0.15625, ((0, 4),)),
        "b_down": scatter_about(splits[15], (D,), 1.5, 6.0, ((0, 4),)),
    }


EPS = 1e-06
GELU_C = 0.7978845608028654

def norm_rows(values):
    centred = values - lax.optimization_barrier(jnp.mean(values, axis=-1, keepdims=True))
    recip = lax.rsqrt(lax.optimization_barrier(jnp.mean(centred * centred, axis=-1, keepdims=True)) + EPS)
    return (centred * recip, recip)

def norm_back(grad, normed, recip):
    return recip * (grad - lax.optimization_barrier(jnp.mean(grad, axis=-1, keepdims=True)) - normed * lax.optimization_barrier(jnp.mean(grad * normed, axis=-1, keepdims=True)))

def gelu_parts(upper):
    inner = GELU_C * (upper + 0.044715 * upper * upper * upper)
    tanh_v = jnp.tanh(inner)
    value = 0.5 * upper * (1.0 + tanh_v)
    slope = 0.5 * (1.0 + tanh_v) + 0.5 * upper * (1.0 - tanh_v * tanh_v) * GELU_C * (1.0 + 3.0 * 0.044715 * upper * upper)
    return (value, slope)

def attention_scores(query, keys):
    return jnp.einsum('bqhd,bkhd->bhqk', query.astype(jnp.float32), keys.astype(jnp.float32)) * (1.0 / math.sqrt(HD))

def layer_forward(latents, cond, weights):
    w_ada, b_ada, w_qkv, b_qv, w_out, b_out, w_up, b_up, w_down, b_down = weights
    batch, length, width = latents.shape
    rows = batch * length
    silu_b = jax.nn.silu(cond).astype(jnp.bfloat16)
    modul = jnp.dot(silu_b, w_ada, preferred_element_type=jnp.float32) + b_ada.astype(jnp.float32)
    shift1, scale1, gate1, shift2, scale2, gate2 = [modul[:, None, i * width:(i + 1) * width] for i in range(6)]
    lat32 = latents.astype(jnp.float32)
    normed1, recip1 = norm_rows(lat32)
    attn_in = (normed1 * (1.0 + scale1) + shift1).astype(jnp.bfloat16).reshape(rows, width)
    bias_full = jnp.concatenate([b_qv[:width].astype(jnp.float32), jnp.zeros((width,), jnp.float32), b_qv[width:].astype(jnp.float32)])
    proj = (jnp.dot(attn_in, w_qkv, preferred_element_type=jnp.float32) + bias_full).astype(jnp.bfloat16)
    split = proj.reshape(batch, length, 3, H, HD)
    query, keys, values = (split[:, :, 0], split[:, :, 1], split[:, :, 2])
    scores = attention_scores(query, keys)
    top = lax.optimization_barrier(jnp.max(scores, axis=-1, keepdims=True))
    lse = top + jnp.log(lax.optimization_barrier(jnp.sum(jnp.exp(scores - top), axis=-1, keepdims=True)))
    probs = jnp.exp(scores - lse).astype(jnp.bfloat16)
    heads_out = jnp.einsum('bhqk,bkhd->bqhd', probs.astype(jnp.float32), values.astype(jnp.float32)).astype(jnp.bfloat16).reshape(rows, width)
    attended = (jnp.dot(heads_out, w_out, preferred_element_type=jnp.float32) + b_out.astype(jnp.float32)).reshape(batch, length, width)
    mid = lat32 + gate1 * attended
    normed2, recip2 = norm_rows(mid)
    mlp_in = (normed2 * (1.0 + scale2) + shift2).astype(jnp.bfloat16).reshape(rows, width)
    upper = jnp.dot(mlp_in, w_up, preferred_element_type=jnp.float32) + b_up.astype(jnp.float32)
    act, slope = gelu_parts(upper)
    act_b = act.astype(jnp.bfloat16)
    down = (jnp.dot(act_b, w_down, preferred_element_type=jnp.float32) + b_down.astype(jnp.float32)).reshape(batch, length, width)
    block_out = mid + gate2 * down
    saved = (cond, silu_b, modul, normed1, recip1, attn_in, query, keys, values, lse, heads_out, attended, normed2, recip2, mlp_in, slope, act_b, down)
    return (block_out, saved)

def layer_backward(cotangent, saved, weights):
    w_ada, b_ada, w_qkv, b_qv, w_out, b_out, w_up, b_up, w_down, b_down = weights
    cond, silu_b, modul, normed1, recip1, attn_in, query, keys, values, lse, heads_out, attended, normed2, recip2, mlp_in, slope, act_b, down = saved
    batch, length, width = normed1.shape
    rows = batch * length
    shift1, scale1, gate1, shift2, scale2, gate2 = [modul[:, None, i * width:(i + 1) * width] for i in range(6)]
    dout = cotangent.astype(jnp.float32)
    dgate2 = lax.optimization_barrier(jnp.sum(dout * down, axis=1))
    dmlp = (dout * gate2).astype(jnp.bfloat16).reshape(rows, width)
    grad_w_down = jnp.dot(act_b.T, dmlp, preferred_element_type=jnp.float32)
    grad_b_down = lax.optimization_barrier(jnp.sum(dmlp.astype(jnp.float32), axis=0))
    dupper = (jnp.dot(dmlp, w_down.T, preferred_element_type=jnp.float32) * slope).astype(jnp.bfloat16)
    grad_w_up = jnp.dot(mlp_in.T, dupper, preferred_element_type=jnp.float32)
    grad_b_up = lax.optimization_barrier(jnp.sum(dupper.astype(jnp.float32), axis=0))
    dmlp_in = jnp.dot(dupper, w_up.T, preferred_element_type=jnp.float32).reshape(batch, length, width)
    dscale2 = lax.optimization_barrier(jnp.sum(dmlp_in * normed2, axis=1))
    dshift2 = lax.optimization_barrier(jnp.sum(dmlp_in, axis=1))
    dmid = dout + norm_back(dmlp_in * (1.0 + scale2), normed2, recip2)
    dgate1 = lax.optimization_barrier(jnp.sum(dmid * attended, axis=1))
    dattn = (dmid * gate1).astype(jnp.bfloat16).reshape(rows, width)
    grad_w_out = jnp.dot(heads_out.T, dattn, preferred_element_type=jnp.float32)
    grad_b_out = lax.optimization_barrier(jnp.sum(dattn.astype(jnp.float32), axis=0))
    dheads = jnp.dot(dattn, w_out.T, preferred_element_type=jnp.float32).astype(jnp.bfloat16).reshape(batch, length, H, HD)
    probs32 = jnp.exp(attention_scores(query, keys) - lse)
    probs_b = probs32.astype(jnp.bfloat16).astype(jnp.float32)
    dvalues = jnp.einsum('bhqk,bqhd->bkhd', probs_b, dheads.astype(jnp.float32))
    dprobs = jnp.einsum('bqhd,bkhd->bhqk', dheads.astype(jnp.float32), values.astype(jnp.float32))
    delta = lax.optimization_barrier(jnp.sum(probs32 * dprobs, axis=-1, keepdims=True))
    dscores = (probs32 * (dprobs - delta)).astype(jnp.bfloat16).astype(jnp.float32)
    scale = 1.0 / math.sqrt(HD)
    dquery = jnp.einsum('bhqk,bkhd->bqhd', dscores, keys.astype(jnp.float32)) * scale
    dkeys = jnp.einsum('bhqk,bqhd->bkhd', dscores, query.astype(jnp.float32)) * scale
    dproj = jnp.stack([dquery, dkeys, dvalues], axis=2).astype(jnp.bfloat16).reshape(rows, 3 * width)
    grad_w_qkv = jnp.dot(attn_in.T, dproj, preferred_element_type=jnp.float32)
    column_sums = lax.optimization_barrier(jnp.sum(dproj.astype(jnp.float32), axis=0))
    grad_b_qv = jnp.concatenate([column_sums[:width], column_sums[2 * width:]])
    dattn_in = jnp.dot(dproj, w_qkv.T, preferred_element_type=jnp.float32).reshape(batch, length, width)
    dscale1 = lax.optimization_barrier(jnp.sum(dattn_in * normed1, axis=1))
    dshift1 = lax.optimization_barrier(jnp.sum(dattn_in, axis=1))
    input_grad = dmid + norm_back(dattn_in * (1.0 + scale1), normed1, recip1)
    dmodul = jnp.concatenate([dshift1, dscale1, dgate1, dshift2, dscale2, dgate2], axis=-1)
    grad_b_ada = lax.optimization_barrier(jnp.sum(dmodul, axis=0))
    grad_w_ada = jnp.dot(silu_b.astype(jnp.float32).T, dmodul, precision=lax.Precision.HIGHEST)
    sig = jax.nn.sigmoid(cond)
    cond_grad = jnp.dot(dmodul, w_ada.astype(jnp.float32).T, precision=lax.Precision.HIGHEST) * (sig * (1.0 + cond * (1.0 - sig)))
    grads = (grad_w_ada, grad_b_ada, grad_w_qkv, grad_b_qv, grad_w_out, grad_b_out, grad_w_up, grad_b_up, grad_w_down, grad_b_down)
    return (input_grad, cond_grad, grads)

def reference(latents, cotangent, timesteps, labels, time_table, class_table, w_ada, b_ada, w_qkv, b_qv, w_out, b_out, w_up, b_up, w_down, b_down):
    weights = (w_ada, b_ada, w_qkv, b_qv, w_out, b_out, w_up, b_up, w_down, b_down)
    cond_all = jnp.take(time_table, timesteps, axis=0) + jnp.take(class_table, labels, axis=0)
    blocks = SEQS // 16
    lat_blocks = latents.reshape(blocks, 16, S, D)
    cot_blocks = cotangent.reshape(blocks, 16, S, D)
    cond_blocks = cond_all.reshape(blocks, 16, D)

    def step(totals, item):
        lat_b, cot_b, cond_b = item
        block_out, saved = layer_forward(lat_b, cond_b, weights)
        input_grad, cond_grad, grads = layer_backward(cot_b, saved, weights)
        totals = tuple((total + grad for total, grad in zip(totals, grads)))
        return (totals, (block_out, input_grad, cond_grad))
    init = tuple((jnp.zeros(w.shape, jnp.float32) for w in weights))
    totals, (outs, in_grads, cond_grads) = lax.scan(step, init, (lat_blocks, cot_blocks, cond_blocks))
    block_out = outs.reshape(SEQS, S, D)
    input_grad = in_grads.reshape(SEQS, S, D)
    cond_grad = cond_grads.reshape(SEQS, D)
    return (block_out, input_grad, cond_grad, totals[0], totals[1], totals[2], totals[3], totals[4], totals[5], totals[6], totals[7], totals[8], totals[9])
```

```python
import functools
import math

import jax
import jax.numpy as jnp
from jax import lax
from jax.experimental import pallas as pl
from jax.experimental.pallas import tpu as pltpu
from jax.sharding import PartitionSpec as P

H = 6
HD = 64
D = 384
TILES = 12
EPS = 1e-06
GELU_C = 0.7978845608028654
MESH = pl.DeviceIdType.MESH
F32 = jnp.float32
BF16 = jnp.bfloat16
MIB = 1024 * 1024


def mm(a, b):
    return lax.dot_general(a, b, (((1,), (0,)), ((), ())), preferred_element_type=F32)


def mm_bt(a, b):
    return lax.dot_general(a, b, (((1,), (1,)), ((), ())), preferred_element_type=F32)


def mm_at(a, b):
    return lax.dot_general(a, b, (((0,), (0,)), ((), ())), preferred_element_type=F32)


def row(vals):
    return jnp.mean(vals, axis=-1, keepdims=True)


def cols(vals):
    return jnp.sum(vals, axis=0, keepdims=True)


def barrier(peers):
    sem = pltpu.get_barrier_semaphore()
    for peer in peers:
        pl.semaphore_signal(sem, inc=1, device_id=peer, device_id_type=MESH)
    pl.semaphore_wait(sem, len(peers))


def remote(src, dst, send, recv, peer):
    return pltpu.make_async_remote_copy(
        src_ref=src, dst_ref=dst, send_sem=send, recv_sem=recv, device_id=peer, device_id_type=MESH
    )


def gather_kernel(
    n, w0, w1, w2, w3, wada, silu, bada, bias,
    o0, o1, o2, o3, omod, obias,
    silu_buf, mod_send, mod_buf, bias_buf,
    g_send, g_recv, f_send, f_recv, s_send, s_recv, m_send, m_recv, b_send, b_recv,
):
    me = lax.axis_index("shard")
    rep = lax.axis_index("rep")
    core = lax.rem(rep, 2)
    sibling = (me, rep + 1 - 2 * core)
    peers = [(lax.rem(me + d, n), rep) for d in range(1, n)]
    barrier(peers + [sibling])

    small = []
    for d in range(1, n):
        peer = peers[d - 1]
        cp = remote(silu.at[peer[0]], silu_buf.at[me], s_send.at[d], s_recv.at[d], peer)
        cp.start()
        bp = remote(bias, bias_buf.at[me], b_send.at[d], b_recv.at[d], peer)
        bp.start()
        small.append((cp, bp))

    mats = [(w0, o0), (w1, o1), (w2, o2), (w3, o3)]
    pushes = {}
    for m, (w, o) in enumerate(mats):
        rows = w.shape[0]
        half = rows // 2
        mine = pl.multiple_of(core * half, 16)
        for d in (1, 3, 2) if n == 4 else range(1, n):
            cp = remote(
                w.at[pl.ds(mine, half)],
                o.at[pl.ds(pl.multiple_of(me * rows + core * half, 16), half)],
                g_send.at[m, d], g_recv.at[m, d], peers[d - 1],
            )
            cp.start()
            pushes[m, d] = cp
    for w, o in mats:
        rows = w.shape[0]
        o[pl.ds(pl.multiple_of(me * rows, 16), rows), :] = w[...]

    silu_buf[me] = silu[me]
    for cp, _ in small:
        cp.wait_recv()
    part = mm(silu_buf[...].reshape(n * 16, silu.shape[2]), wada[...])
    bada_v = bada[...]
    for p in range(n):
        mod_send[p] = part[p * 16 : p * 16 + 8] + bada_v
    mods = []
    for d in range(1, n):
        peer = peers[d - 1]
        cp = remote(mod_send.at[peer[0]], mod_buf.at[me], m_send.at[d], m_recv.at[d], peer)
        cp.start()
        mods.append(cp)
    mod_buf[me] = mod_send[me]
    bias_buf[me] = bias[...]
    for _, bp in small:
        bp.wait_recv()
    total = bias_buf[0]
    for p in range(1, n):
        total = total + bias_buf[p]
    obias[...] = total
    for cp in mods:
        cp.wait_recv()
    total = mod_buf[0]
    for p in range(1, n):
        total = total + mod_buf[p]
    omod[...] = total

    passed = []
    for m, (w, o) in enumerate(mats):
        rows = w.shape[0]
        half = rows // 2
        for d in (1, 3, 2) if n == 4 else range(1, n):
            pushes[m, d].wait_recv()
            origin = lax.rem(me - d + n, n)
            spot = pl.ds(pl.multiple_of(origin * rows + core * half, 16), half)
            cp = remote(o.at[spot], o.at[spot], f_send.at[m, d], f_recv.at[m, d], sibling)
            cp.start()
            passed.append(cp)
    for cp in passed:
        cp.wait()
    for cp in pushes.values():
        cp.wait_send()
    for cp, bp in small:
        cp.wait_send()
        bp.wait_send()
    for cp in mods:
        cp.wait_send()


def gather_weights(n, w_qkv, w_out, w_up, w_down, w_ada, silu, bada, bias):
    mats = (w_qkv, w_out, w_up, w_down)
    vmem = pl.BlockSpec(memory_space=pltpu.VMEM)
    dma = pltpu.SemaphoreType.DMA
    return pl.pallas_call(
        functools.partial(gather_kernel, n),
        out_shape=[jax.ShapeDtypeStruct((n * w.shape[0], w.shape[1]), BF16) for w in mats]
        + [jax.ShapeDtypeStruct(bada.shape[:0] + (8, bada.shape[1]), F32), jax.ShapeDtypeStruct(bias.shape, F32)],
        in_specs=[vmem] * 8,
        out_specs=[vmem] * 6,
        scratch_shapes=[
            pltpu.VMEM(silu.shape, BF16),
            pltpu.VMEM((n, 8, bada.shape[1]), F32),
            pltpu.VMEM((n, 8, bada.shape[1]), F32),
            pltpu.VMEM((n,) + bias.shape, F32),
            dma((4, n)), dma((4, n)), dma((4, n)), dma((4, n)),
            dma((n,)), dma((n,)), dma((n,)), dma((n,)), dma((n,)), dma((n,)),
        ],
        compiler_params=pltpu.CompilerParams(
            collective_id=0, has_side_effects=True, vmem_limit_bytes=32 * MIB
        ),
        name="gather_weights",
    )(*mats, w_ada, silu, bada, bias)


def block_kernel(
    lat_ref, cot_ref, mod_ref, bias_ref, wqkv, wout, wup, wdown,
    out_ref, ing_ref, dmod_ref, pg_ref, gb_ref,
    acc, proj_s, prob_s, heads_s, act_s, slope_s, dproj_s,
):
    step = pl.program_id(0)
    last = pl.num_programs(0) - 1

    @pl.when(step == 0)
    def _():
        acc[...] = jnp.zeros_like(acc)
        gb_ref[...] = jnp.zeros_like(gb_ref)

    mod = mod_ref[0]
    shift1, scale1, gate1, shift2, scale2, gate2 = [mod[i : i + 1] for i in range(6)]
    bias = bias_ref[...]
    lat = lat_ref[0].astype(F32)
    centred = lat - row(lat)
    recip1 = lax.rsqrt(row(centred * centred) + EPS)
    normed1 = centred * recip1
    attn_in = (normed1 * (1.0 + scale1) + shift1).astype(BF16)
    for j in range(3):
        part = mm(attn_in, wqkv[:, j * D : (j + 1) * D])
        if j == 0:
            part = part + bias[0:1]
        if j == 2:
            part = part + bias[1:2]
        proj_s[:, j * D : (j + 1) * D] = part.astype(BF16)

    low = lax.broadcasted_iota(jnp.int32, (256, 128), 1) < HD
    zero = jnp.zeros((256, 128), BF16)
    scale = 1.0 / math.sqrt(HD)
    for pair in range(H // 2):
        at = pair * 128
        q = proj_s[:, at : at + 128]
        k = proj_s[:, D + at : D + at + 128]
        v = proj_s[:, 2 * D + at : 2 * D + at + 128]
        outs = []
        for side in range(2):
            qm = jnp.where(low, q, zero) if side == 0 else jnp.where(low, zero, q)
            s = mm_bt(qm, k) * scale
            e = jnp.exp(s - jnp.max(s, axis=-1, keepdims=True))
            p = e * (1.0 / jnp.sum(e, axis=-1, keepdims=True))
            prob_s[2 * pair + side] = p
            outs.append(mm(p.astype(BF16), v))
        heads_s[:, at : at + 128] = jnp.where(low, outs[0], outs[1]).astype(BF16)

    attended = mm(heads_s[...], wout[...]) + bias[2:3]
    mid = lat + gate1 * attended
    centred = mid - row(mid)
    recip2 = lax.rsqrt(row(centred * centred) + EPS)
    normed2 = centred * recip2
    mlp_in = (normed2 * (1.0 + scale2) + shift2).astype(BF16)
    down = jnp.zeros((256, D), F32)
    for j in range(4):
        at = slice(j * D, (j + 1) * D)
        u = mm(mlp_in, wup[:, at]) + bias[3 + j : 4 + j]
        sq = u * u
        t = jnp.tanh(GELU_C * u * (1.0 + 0.044715 * sq))
        half = 0.5 * (1.0 + t)
        act = (u * half).astype(BF16)
        act_s[:, at] = act
        slope_s[:, at] = half + 0.5 * u * (1.0 - t * t) * (GELU_C + 3.0 * 0.044715 * GELU_C * sq)
        down = down + mm(act, wdown[at, :])
    down = down + bias[7:8]
    out_ref[0] = mid + gate2 * down

    dout = cot_ref[0].astype(F32)
    dmod_ref[0, 5:6, :] = cols(dout * down)
    dmlp = (dout * gate2).astype(BF16)
    gb_ref[7:8, :] += cols(dmlp.astype(F32))
    dmlp_in = jnp.zeros((256, D), F32)
    for j in range(4):
        at = slice(j * D, (j + 1) * D)
        acc[8 + j] += mm_at(act_s[:, at], dmlp)
        dup = (mm_bt(dmlp, wdown[at, :]) * slope_s[:, at]).astype(BF16)
        gb_ref[3 + j : 4 + j, :] += cols(dup.astype(F32))
        acc[4 + j] += mm_at(mlp_in, dup)
        dmlp_in = dmlp_in + mm_bt(dup, wup[:, at])
    dmod_ref[0, 4:5, :] = cols(dmlp_in * normed2)
    dmod_ref[0, 3:4, :] = cols(dmlp_in)
    g2 = dmlp_in * (1.0 + scale2)
    dmid = dout + recip2 * (g2 - row(g2) - normed2 * row(g2 * normed2))
    dmod_ref[0, 2:3, :] = cols(dmid * attended)
    dattn = (dmid * gate1).astype(BF16)
    gb_ref[2:3, :] += cols(dattn.astype(F32))
    acc[3] += mm_at(heads_s[...], dattn)
    dheads = mm_bt(dattn, wout[...]).astype(BF16)
    for pair in range(H // 2):
        at = pair * 128
        q = proj_s[:, at : at + 128]
        k = proj_s[:, D + at : D + at + 128]
        v = proj_s[:, 2 * D + at : 2 * D + at + 128]
        dh = dheads[:, at : at + 128]
        dqs, dks, dvs = [], [], []
        for side in range(2):
            p = prob_s[2 * pair + side]
            dhm = jnp.where(low, dh, zero) if side == 0 else jnp.where(low, zero, dh)
            dvs.append(mm_at(p.astype(BF16), dh))
            dp = mm_bt(dhm, v)
            delta = jnp.sum(p * dp, axis=-1, keepdims=True)
            ds = (p * (dp - delta)).astype(BF16)
            dqs.append(mm(ds, k))
            dks.append(mm_at(ds, q))
        dproj_s[:, at : at + 128] = (jnp.where(low, dqs[0], dqs[1]) * scale).astype(BF16)
        dproj_s[:, D + at : D + at + 128] = (jnp.where(low, dks[0], dks[1]) * scale).astype(BF16)
        dproj_s[:, 2 * D + at : 2 * D + at + 128] = jnp.where(low, dvs[0], dvs[1]).astype(BF16)
    dattn_in = jnp.zeros((256, D), F32)
    for j in range(3):
        at = slice(j * D, (j + 1) * D)
        dpj = dproj_s[:, at]
        acc[j] += mm_at(attn_in, dpj)
        dattn_in = dattn_in + mm_bt(dpj, wqkv[:, at])
        if j != 1:
            gb_ref[j // 2 : j // 2 + 1, :] += cols(dpj.astype(F32))
    dmod_ref[0, 1:2, :] = cols(dattn_in * normed1)
    dmod_ref[0, 0:1, :] = cols(dattn_in)
    g1 = dattn_in * (1.0 + scale1)
    ing_ref[0] = dmid + recip1 * (g1 - row(g1) - normed1 * row(g1 * normed1))

    @pl.when(step == last)
    def _():
        for s in range(4):
            for t in range(8):
                pg_ref[s, t * 96 : (t + 1) * 96, :] = acc[t, s * 96 : (s + 1) * 96, :].astype(BF16)
            pg_ref[s, 768:1152, :] = acc[8 + s].astype(BF16)


def run_block(latents, cotangent, modul, bias, wqkv, wout, wup, wdown):
    batch, length, width = latents.shape
    tok = pl.BlockSpec((1, length, width), lambda i: (i, 0, 0))
    mod = pl.BlockSpec((1, 6, width), lambda i: (i, 0, 0))
    whole = pl.BlockSpec(memory_space=pltpu.VMEM)
    return pl.pallas_call(
        block_kernel,
        grid=(batch,),
        in_specs=[tok, tok, mod] + [whole] * 5,
        out_specs=[tok, tok, mod, whole, whole],
        out_shape=[
            jax.ShapeDtypeStruct(latents.shape, F32),
            jax.ShapeDtypeStruct(latents.shape, F32),
            jax.ShapeDtypeStruct((batch, 6, width), F32),
            jax.ShapeDtypeStruct((4, 96 * TILES, width), BF16),
            jax.ShapeDtypeStruct((8, width), F32),
        ],
        scratch_shapes=[
            pltpu.VMEM((TILES, D, D), F32),
            pltpu.VMEM((length, 3 * D), BF16),
            pltpu.VMEM((H, length, length), F32),
            pltpu.VMEM((length, D), BF16),
            pltpu.VMEM((length, 4 * D), BF16),
            pltpu.VMEM((length, 4 * D), F32),
            pltpu.VMEM((length, 3 * D), BF16),
        ],
        compiler_params=pltpu.CompilerParams(
            dimension_semantics=("arbitrary",), vmem_limit_bytes=48 * MIB
        ),
        cost_estimate=pl.CostEstimate(flops=9 * 10**9, bytes_accessed=12 * 10**6, transcendentals=2 * 10**6),
        name="block",
    )(latents, cotangent, modul, bias, wqkv, wout, wup, wdown)


def reduce_kernel(
    n, nz, pg, pay, out, pays,
    sib_buf, chip, grp_buf, mine, z_buf,
    a_send, a_recv, b_send, b_recv, c_send, c_recv, d_send, d_recv, e_send, e_recv,
    pz_send, pz_recv, ps_send, ps_recv, pc_send, pc_recv,
):
    me = lax.axis_index("shard")
    rep = lax.axis_index("rep")
    core = lax.rem(rep, 2)
    z = rep // 2
    sibling = (me, rep + 1 - 2 * core)
    speers = [(lax.rem(me + d, n), rep) for d in range(1, n)]
    zs = [lax.rem(z + d, nz) for d in range(nz)]
    zpeers = [(me, zs[d] * 2 + core) for d in range(1, nz)]
    barrier([sibling] + speers + zpeers)
    half = pg.shape[1] // 2
    chunk = half // nz
    own = pl.ds(pl.multiple_of(core * half, 16), half)
    other = pl.ds(pl.multiple_of((1 - core) * half, 16), half)

    order = [1, 3, 2, 0] if n == 4 else list(range(1, n)) + [0]
    firsts = {}
    for d in order:
        s = lax.rem(me + d, n)
        cp = remote(pg.at[s, other], sib_buf.at[s], a_send.at[d], a_recv.at[d], sibling)
        cp.start()
        firsts[d] = cp
    pz = []
    for d in range(1, nz):
        cp = remote(pay, pays.at[core, me, z], pz_send.at[d], pz_recv.at[d], zpeers[d - 1])
        cp.start()
        pz.append(cp)
    pays[core, me, z] = pay[...]
    seconds = {}
    for d in order:
        s = lax.rem(me + d, n)
        firsts[d].wait_recv()
        both = pg[s, own, :].astype(F32) + sib_buf[s].astype(F32)
        chip[s] = both.astype(BF16)
        if d:
            cp = remote(chip.at[s], grp_buf.at[me], b_send.at[d], b_recv.at[d], speers[d - 1])
            cp.start()
            seconds[d] = cp
    for cp in pz:
        cp.wait_recv()
    ps = []
    for d in range(1, n):
        cp = remote(pays.at[core, me], pays.at[core, me], ps_send.at[d], ps_recv.at[d], speers[d - 1])
        cp.start()
        ps.append(cp)
    for d in range(1, n):
        seconds[d].wait_recv()
    total = chip[me].astype(F32)
    for d in range(1, n):
        total = total + grp_buf[lax.rem(me + d, n)].astype(F32)
    mine[...] = total.astype(BF16)
    thirds = []
    for d in range(1, nz):
        spot = pl.ds(pl.multiple_of(zs[d] * chunk, 16), chunk)
        cp = remote(mine.at[spot], z_buf.at[z], c_send.at[d], c_recv.at[d], zpeers[d - 1])
        cp.start()
        thirds.append(cp)
    for cp in ps:
        cp.wait_recv()
    pc = remote(pays.at[core], pays.at[core], pc_send, pc_recv, sibling)
    pc.start()
    for cp in thirds:
        cp.wait_recv()
    total = mine[pl.ds(pl.multiple_of(z * chunk, 16), chunk), :].astype(F32)
    for d in range(1, nz):
        total = total + z_buf[zs[d]].astype(F32)
    spot = pl.ds(pl.multiple_of(core * half + z * chunk, 16), chunk)
    out[spot, :] = total.astype(BF16)
    fourths = []
    for d in range(1, nz):
        cp = remote(out.at[spot], out.at[spot], d_send.at[d], d_recv.at[d], zpeers[d - 1])
        cp.start()
        fourths.append(cp)
    fifths = [remote(out.at[spot], out.at[spot], e_send.at[0], e_recv.at[0], sibling)]
    fifths[0].start()
    for d in range(1, nz):
        fourths[d - 1].wait_recv()
        origin = lax.rem(z - d + nz, nz)
        spot = pl.ds(pl.multiple_of(core * half + origin * chunk, 16), chunk)
        cp = remote(out.at[spot], out.at[spot], e_send.at[d], e_recv.at[d], sibling)
        cp.start()
        fifths.append(cp)
    for cp in fifths:
        cp.wait()
    pc.wait()
    for cp in list(firsts.values()) + list(seconds.values()) + thirds + fourths + pz + ps:
        cp.wait_send()


def reduce_grads(n, nz, pg, pay):
    vmem = pl.BlockSpec(memory_space=pltpu.VMEM)
    dma = pltpu.SemaphoreType.DMA
    rows, width = pg.shape[1:]
    half = rows // 2
    return pl.pallas_call(
        functools.partial(reduce_kernel, n, nz),
        out_shape=[
            jax.ShapeDtypeStruct((rows, width), BF16),
            jax.ShapeDtypeStruct((2, n, nz) + pay.shape, BF16),
        ],
        in_specs=[vmem] * 2,
        out_specs=[vmem] * 2,
        scratch_shapes=[
            pltpu.VMEM((n, half, width), BF16),
            pltpu.VMEM((n, half, width), BF16),
            pltpu.VMEM((n, half, width), BF16),
            pltpu.VMEM((half, width), BF16),
            pltpu.VMEM((nz, half // nz, width), BF16),
            dma((n,)), dma((n,)), dma((n,)), dma((n,)),
            dma((nz,)), dma((nz,)), dma((nz,)), dma((nz,)), dma((nz,)), dma((nz,)),
            dma((nz,)), dma((nz,)), dma((n,)), dma((n,)), dma, dma,
        ],
        compiler_params=pltpu.CompilerParams(
            collective_id=1, has_side_effects=True, vmem_limit_bytes=40 * MIB
        ),
        name="reduce_grads",
    )(pg, pay)


def place(piece, n, me):
    full = jnp.zeros((n * piece.shape[0],), F32)
    return lax.dynamic_update_slice(full, piece.astype(F32), (me * piece.shape[0],))


def body(
    n, reps,
    latents, cotangent, timesteps, labels, time_table, class_table,
    w_ada, b_ada, w_qkv, b_qv, w_out, b_out, w_up, b_up, w_down, b_down,
):
    me = lax.axis_index("shard")
    batch, length, width = latents.shape
    cond = jnp.concatenate(
        [
            lax.dynamic_slice(time_table, (timesteps[i], 0), (1, width))
            + lax.dynamic_slice(class_table, (labels[i], 0), (1, width))
            for i in range(batch)
        ]
    )
    sig = jax.nn.sigmoid(cond)
    silu_b = (cond * sig).astype(BF16)
    share = width // n
    silu = jnp.pad(
        silu_b.reshape(batch, n, share).transpose(1, 0, 2), ((0, 0), (0, 16 - batch), (0, 0))
    )
    bias = jnp.concatenate(
        [place(b_qv, n, me), place(b_out, n, me), place(b_up, n, me), place(b_down, n, me)]
    ).reshape(8, width)
    wqkv, wout, wup, wdown, modul, bias = gather_weights(
        n, w_qkv, w_out, w_up, w_down, w_ada, silu, place(b_ada, n, me)[None, :], bias
    )
    w_late, _ = lax.optimization_barrier((w_ada, modul))
    w_ada_full = lax.all_gather(w_late, "shard", axis=0, tiled=True)
    block_out, input_grad, dmod, pg, gb = run_block(
        latents, cotangent, modul[:batch].reshape(batch, 6, width), bias, wqkv, wout, wup, wdown
    )
    cond_grad = jnp.dot(
        dmod.reshape(batch, 6 * width), w_ada_full.astype(F32).T, precision=lax.Precision.HIGHEST
    ) * (sig * (1.0 + cond * (1.0 - sig)))

    used = batch * 7 + 8
    pay = jnp.concatenate(
        [
            dmod.reshape(batch * 6, width),
            silu_b.astype(F32),
            gb,
            jnp.zeros((-used % 16, width), F32),
        ]
    ).astype(BF16)
    nz = reps // 2
    if reps % 2 == 0 and pg.shape[1] % (32 * nz) == 0:
        own, pays = reduce_grads(n, nz, pg, pay)
        own = own.astype(F32)
    else:
        own = lax.psum(lax.psum_scatter(pg.astype(F32), "shard", scatter_dimension=0), "rep")
        pays = lax.all_gather(pay, ("shard", "rep"))
    pays = pays.reshape((-1,) + pay.shape)
    count = pays.shape[0] * batch
    dm = pays[:, : batch * 6].reshape(count, 6 * width)
    silu_all = pays[:, batch * 6 : batch * 7].reshape(count, width)
    silu_own = lax.dynamic_slice(silu_all, (0, me * share), (count, share))
    grad_w_ada = mm_at(silu_own, dm)
    grad_b_ada = jnp.sum(dm.astype(F32), axis=0)
    gbs = jnp.sum(pays[:, batch * 7 : used].astype(F32), axis=0).reshape(-1)

    def take(vec):
        size = vec.shape[0] // n
        return lax.dynamic_slice(vec, (me * size,), (size,))

    tiles = [own[t * 96 : (t + 1) * 96] for t in range(8)]
    return (
        block_out,
        input_grad,
        cond_grad,
        grad_w_ada,
        take(grad_b_ada),
        jnp.concatenate(tiles[0:3], axis=1),
        take(gbs[: 2 * width]),
        tiles[3],
        take(gbs[2 * width : 3 * width]),
        jnp.concatenate(tiles[4:8], axis=1),
        take(gbs[3 * width : 7 * width]),
        own[768:],
        take(gbs[7 * width :]),
    )


def solution(mesh):
    both = ("shard", "rep")
    placed = (P(both, None, None), P(both, None, None), P(both), P(both), P(), P()) + (
        P("shard", None),
        P("shard"),
    ) * 5
    return jax.shard_map(
        functools.partial(body, mesh.shape["shard"], mesh.shape["rep"]),
        mesh=mesh,
        in_specs=placed,
        out_specs=(P(both, None, None), P(both, None, None), P(both, None))
        + (P("shard", None), P("shard")) * 5,
        check_vma=False,
    )
```

```python
import functools
import math

import jax
import jax.numpy as jnp
from jax import lax
from jax.experimental import pallas as pl
from jax.experimental.pallas import tpu as pltpu
from jax.sharding import PartitionSpec as P

H = 6
HD = 64
D = 384
TILES = 12
PIECES = 3
EPS = 1e-06
GELU_C = 0.7978845608028654
MESH = pl.DeviceIdType.MESH
F32 = jnp.float32
BF16 = jnp.bfloat16
MIB = 1024 * 1024


def mm(a, b):
    return lax.dot_general(a, b, (((1,), (0,)), ((), ())), preferred_element_type=F32)


def mm_bt(a, b):
    return lax.dot_general(a, b, (((1,), (1,)), ((), ())), preferred_element_type=F32)


def mm_at(a, b):
    return lax.dot_general(a, b, (((0,), (0,)), ((), ())), preferred_element_type=F32)


def row(vals):
    return jnp.mean(vals, axis=-1, keepdims=True)


def cols(vals):
    return jnp.sum(vals, axis=0, keepdims=True)


def barrier(peers):
    sem = pltpu.get_barrier_semaphore()
    for peer in peers:
        pl.semaphore_signal(sem, inc=1, device_id=peer, device_id_type=MESH)
    pl.semaphore_wait(sem, len(peers))


def remote(src, dst, send, recv, peer):
    return pltpu.make_async_remote_copy(
        src_ref=src, dst_ref=dst, send_sem=send, recv_sem=recv, device_id=peer, device_id_type=MESH
    )


def gather_kernel(
    n, w0, w1, w2, w3, wada, silu, bada, bias,
    o0, o1, o2, o3, omod, obias,
    silu_buf, mod_send, mod_buf, bias_buf, l_sem,
    g_send, g_recv, f_send, f_recv, s_send, s_recv, m_send, m_recv, b_send, b_recv,
):
    me = lax.axis_index("shard")
    rep = lax.axis_index("rep")
    core = lax.rem(rep, 2)
    sibling = (me, rep + 1 - 2 * core)
    peers = [(lax.rem(me + d, n), rep) for d in range(1, n)]
    barrier(peers + [sibling])

    small = []
    for d in range(1, n):
        peer = peers[d - 1]
        cp = remote(silu.at[peer[0]], silu_buf.at[me], s_send.at[d], s_recv.at[d], peer)
        cp.start()
        bp = remote(bias, bias_buf.at[me], b_send.at[d], b_recv.at[d], peer)
        bp.start()
        small.append((cp, bp))

    mats = [(w0, o0), (w1, o1), (w2, o2), (w3, o3)]
    pushes = {}
    for m, (w, o) in enumerate(mats):
        rows = w.shape[0]
        half = rows // 2
        mine = pl.multiple_of(core * half, 16)
        for d in (1, 3, 2) if n == 4 else range(1, n):
            cp = remote(
                w.at[pl.ds(mine, half)],
                o.at[pl.ds(pl.multiple_of(me * rows + core * half, 16), half)],
                g_send.at[m, d], g_recv.at[m, d], peers[d - 1],
            )
            cp.start()
            pushes[m, d] = cp
    locals_ = []
    for m, (w, o) in enumerate(mats):
        rows = w.shape[0]
        cp = pltpu.make_async_copy(w, o.at[pl.ds(pl.multiple_of(me * rows, 16), rows)], l_sem.at[m])
        cp.start()
        locals_.append(cp)

    silu_buf[me] = silu[me]
    for cp, _ in small:
        cp.wait_recv()
    part = mm(silu_buf[...].reshape(n * 16, silu.shape[2]), wada[...])
    bada_v = bada[...]
    for p in range(n):
        mod_send[p] = part[p * 16 : p * 16 + 8] + bada_v
    mods = []
    for d in range(1, n):
        peer = peers[d - 1]
        cp = remote(mod_send.at[peer[0]], mod_buf.at[me], m_send.at[d], m_recv.at[d], peer)
        cp.start()
        mods.append(cp)
    mod_buf[me] = mod_send[me]
    bias_buf[me] = bias[...]
    for _, bp in small:
        bp.wait_recv()
    total = bias_buf[0]
    for p in range(1, n):
        total = total + bias_buf[p]
    obias[...] = total
    for cp in mods:
        cp.wait_recv()
    total = mod_buf[0]
    for p in range(1, n):
        total = total + mod_buf[p]
    omod[...] = total

    passed = []
    for m, (w, o) in enumerate(mats):
        rows = w.shape[0]
        half = rows // 2
        for d in (1, 3, 2) if n == 4 else range(1, n):
            pushes[m, d].wait_recv()
            origin = lax.rem(me - d + n, n)
            spot = pl.ds(pl.multiple_of(origin * rows + core * half, 16), half)
            cp = remote(o.at[spot], o.at[spot], f_send.at[m, d], f_recv.at[m, d], sibling)
            cp.start()
            passed.append(cp)
    for cp in passed + locals_:
        cp.wait()
    for cp in pushes.values():
        cp.wait_send()
    for cp, bp in small:
        cp.wait_send()
        bp.wait_send()
    for cp in mods:
        cp.wait_send()


def gather_weights(n, w_qkv, w_out, w_up, w_down, w_ada, silu, bada, bias):
    mats = (w_qkv, w_out, w_up, w_down)
    vmem = pl.BlockSpec(memory_space=pltpu.VMEM)
    hbm = pl.BlockSpec(memory_space=pl.ANY)
    dma = pltpu.SemaphoreType.DMA
    return pl.pallas_call(
        functools.partial(gather_kernel, n),
        out_shape=[jax.ShapeDtypeStruct((n * w.shape[0], w.shape[1]), BF16) for w in mats]
        + [jax.ShapeDtypeStruct((8, bada.shape[1]), F32), jax.ShapeDtypeStruct(bias.shape, F32)],
        in_specs=[hbm] * 4 + [vmem] * 4,
        out_specs=[hbm] * 4 + [vmem] * 2,
        scratch_shapes=[
            pltpu.VMEM(silu.shape, BF16),
            pltpu.VMEM((n, 8, bada.shape[1]), F32),
            pltpu.VMEM((n, 8, bada.shape[1]), F32),
            pltpu.VMEM((n,) + bias.shape, F32),
            dma((4,)), dma((4, n)), dma((4, n)), dma((4, n)), dma((4, n)),
            dma((n,)), dma((n,)), dma((n,)), dma((n,)), dma((n,)), dma((n,)),
        ],
        compiler_params=pltpu.CompilerParams(
            collective_id=0, has_side_effects=True, vmem_limit_bytes=58 * MIB
        ),
        name="gather_weights",
    )(*mats, w_ada, silu, bada, bias)


def block_kernel(
    lat_ref, cot_ref, mod_ref, bias_ref, silu_ref, wqkv, wout, wup, wdown,
    out_ref, ing_ref, dmod_ref, pg_ref, pay_ref,
    gb_ref, dm_s, acc, proj_s, prob_s, heads_s, act_s, slope_s, dproj_s,
):
    step = pl.program_id(0)
    last = pl.num_programs(0) - 1

    @pl.when(step == 0)
    def _():
        acc[...] = jnp.zeros_like(acc)
        gb_ref[...] = jnp.zeros_like(gb_ref)

    mod = mod_ref[0]
    shift1, scale1, gate1, shift2, scale2, gate2 = [mod[i : i + 1] for i in range(6)]
    bias = bias_ref[...]
    lat = lat_ref[0].astype(F32)
    centred = lat - row(lat)
    recip1 = lax.rsqrt(row(centred * centred) + EPS)
    normed1 = centred * recip1
    attn_in = (normed1 * (1.0 + scale1) + shift1).astype(BF16)
    for j in range(3):
        part = mm(attn_in, wqkv[:, j * D : (j + 1) * D])
        if j == 0:
            part = part + bias[0:1]
        if j == 2:
            part = part + bias[1:2]
        proj_s[:, j * D : (j + 1) * D] = part.astype(BF16)

    low = lax.broadcasted_iota(jnp.int32, (256, 128), 1) < HD
    zero = jnp.zeros((256, 128), BF16)
    scale = 1.0 / math.sqrt(HD)
    for pair in range(H // 2):
        at = pair * 128
        q = proj_s[:, at : at + 128]
        k = proj_s[:, D + at : D + at + 128]
        v = proj_s[:, 2 * D + at : 2 * D + at + 128]
        outs = []
        for side in range(2):
            qm = jnp.where(low, q, zero) if side == 0 else jnp.where(low, zero, q)
            s = mm_bt(qm, k) * scale
            e = jnp.exp(s - jnp.max(s, axis=-1, keepdims=True))
            p = e * (1.0 / jnp.sum(e, axis=-1, keepdims=True))
            prob_s[2 * pair + side] = p
            outs.append(mm(p.astype(BF16), v))
        heads_s[:, at : at + 128] = jnp.where(low, outs[0], outs[1]).astype(BF16)

    attended = mm(heads_s[...], wout[...]) + bias[2:3]
    mid = lat + gate1 * attended
    centred = mid - row(mid)
    recip2 = lax.rsqrt(row(centred * centred) + EPS)
    normed2 = centred * recip2
    mlp_in = (normed2 * (1.0 + scale2) + shift2).astype(BF16)
    down = jnp.zeros((256, D), F32)
    for j in range(4):
        at = slice(j * D, (j + 1) * D)
        u = mm(mlp_in, wup[:, at]) + bias[3 + j : 4 + j]
        sq = u * u
        t = jnp.tanh(GELU_C * u * (1.0 + 0.044715 * sq))
        half = 0.5 * (1.0 + t)
        act = (u * half).astype(BF16)
        act_s[:, at] = act
        slope_s[:, at] = half + 0.5 * u * (1.0 - t * t) * (GELU_C + 3.0 * 0.044715 * GELU_C * sq)
        down = down + mm(act, wdown[at, :])
    down = down + bias[7:8]
    out_ref[0] = mid + gate2 * down

    dout = cot_ref[0].astype(F32)
    dmod_ref[0, 5:6, :] = cols(dout * down)
    dmlp = (dout * gate2).astype(BF16)
    gb_ref[7:8, :] += cols(dmlp.astype(F32))
    dmlp_in = jnp.zeros((256, D), F32)
    for j in range(4):
        at = slice(j * D, (j + 1) * D)
        acc[8 + j] += mm_at(act_s[:, at], dmlp)
        dup = (mm_bt(dmlp, wdown[at, :]) * slope_s[:, at]).astype(BF16)
        gb_ref[3 + j : 4 + j, :] += cols(dup.astype(F32))
        acc[4 + j] += mm_at(mlp_in, dup)
        dmlp_in = dmlp_in + mm_bt(dup, wup[:, at])
    dmod_ref[0, 4:5, :] = cols(dmlp_in * normed2)
    dmod_ref[0, 3:4, :] = cols(dmlp_in)
    g2 = dmlp_in * (1.0 + scale2)
    dmid = dout + recip2 * (g2 - row(g2) - normed2 * row(g2 * normed2))
    dmod_ref[0, 2:3, :] = cols(dmid * attended)
    dattn = (dmid * gate1).astype(BF16)
    gb_ref[2:3, :] += cols(dattn.astype(F32))
    acc[3] += mm_at(heads_s[...], dattn)
    dheads = mm_bt(dattn, wout[...]).astype(BF16)
    for pair in range(H // 2):
        at = pair * 128
        q = proj_s[:, at : at + 128]
        k = proj_s[:, D + at : D + at + 128]
        v = proj_s[:, 2 * D + at : 2 * D + at + 128]
        dh = dheads[:, at : at + 128]
        dqs, dks, dvs = [], [], []
        for side in range(2):
            p = prob_s[2 * pair + side]
            dhm = jnp.where(low, dh, zero) if side == 0 else jnp.where(low, zero, dh)
            dvs.append(mm_at(p.astype(BF16), dh))
            dp = mm_bt(dhm, v)
            delta = jnp.sum(p * dp, axis=-1, keepdims=True)
            ds = (p * (dp - delta)).astype(BF16)
            dqs.append(mm(ds, k))
            dks.append(mm_at(ds, q))
        dproj_s[:, at : at + 128] = (jnp.where(low, dqs[0], dqs[1]) * scale).astype(BF16)
        dproj_s[:, D + at : D + at + 128] = (jnp.where(low, dks[0], dks[1]) * scale).astype(BF16)
        dproj_s[:, 2 * D + at : 2 * D + at + 128] = jnp.where(low, dvs[0], dvs[1]).astype(BF16)
    dattn_in = jnp.zeros((256, D), F32)
    for j in range(3):
        at = slice(j * D, (j + 1) * D)
        dpj = dproj_s[:, at]
        acc[j] += mm_at(attn_in, dpj)
        dattn_in = dattn_in + mm_bt(dpj, wqkv[:, at])
        if j != 1:
            gb_ref[j // 2 : j // 2 + 1, :] += cols(dpj.astype(F32))
    dmod_ref[0, 1:2, :] = cols(dattn_in * normed1)
    dmod_ref[0, 0:1, :] = cols(dattn_in)
    g1 = dattn_in * (1.0 + scale1)
    ing_ref[0] = dmid + recip1 * (g1 - row(g1) - normed1 * row(g1 * normed1))

    for j in range(6):
        dm_s[pl.ds(step * 6 + j, 1), :] = dmod_ref[0, j : j + 1, :]

    @pl.when(step == last)
    def _():
        batch = silu_ref.shape[0]
        fill = pay_ref.shape[0] - 7 * batch - 8
        pay_ref[...] = jnp.concatenate(
            [dm_s[...], silu_ref[...], gb_ref[...], jnp.zeros((fill, D), F32)]
        ).astype(BF16)
        for s in range(4):
            for t in range(8):
                pg_ref[s, t * 96 : (t + 1) * 96, :] = acc[t, s * 96 : (s + 1) * 96, :].astype(BF16)
            pg_ref[s, 768:1152, :] = acc[8 + s].astype(BF16)


def run_block(latents, cotangent, modul, bias, silu, wqkv, wout, wup, wdown):
    batch, length, width = latents.shape
    tok = pl.BlockSpec((1, length, width), lambda i: (i, 0, 0))
    mod = pl.BlockSpec((1, 6, width), lambda i: (i, 0, 0))
    whole = pl.BlockSpec(memory_space=pltpu.VMEM)
    rows = 7 * batch + 8

    def full(a):
        return pl.BlockSpec(a.shape, lambda i: (0, 0))

    return pl.pallas_call(
        block_kernel,
        grid=(batch,),
        in_specs=[tok, tok, mod] + [full(a) for a in (bias, silu, wqkv, wout, wup, wdown)],
        out_specs=[tok, tok, mod, whole, whole],
        out_shape=[
            jax.ShapeDtypeStruct(latents.shape, F32),
            jax.ShapeDtypeStruct(latents.shape, F32),
            jax.ShapeDtypeStruct((batch, 6, width), F32),
            jax.ShapeDtypeStruct((4, 96 * TILES, width), BF16),
            jax.ShapeDtypeStruct((rows + -rows % 16, width), BF16),
        ],
        scratch_shapes=[
            pltpu.VMEM((8, width), F32),
            pltpu.VMEM((6 * batch, width), F32),
            pltpu.VMEM((TILES, D, D), F32),
            pltpu.VMEM((length, 3 * D), BF16),
            pltpu.VMEM((H, length, length), F32),
            pltpu.VMEM((length, D), BF16),
            pltpu.VMEM((length, 4 * D), BF16),
            pltpu.VMEM((length, 4 * D), F32),
            pltpu.VMEM((length, 3 * D), BF16),
        ],
        compiler_params=pltpu.CompilerParams(
            dimension_semantics=("arbitrary",), vmem_limit_bytes=58 * MIB
        ),
        cost_estimate=pl.CostEstimate(flops=9 * 10**9, bytes_accessed=12 * 10**6, transcendentals=2 * 10**6),
        name="block",
    )(latents, cotangent, modul, bias, silu, wqkv, wout, wup, wdown)


def reduce_kernel(
    n, nz, pg, pay, out, pays,
    sib_buf, chip, grp_buf, mine, z_buf,
    a_send, a_recv, b_send, b_recv, c_send, c_recv, d_send, d_recv, e_send, e_recv,
    pz_send, pz_recv, ps_send, ps_recv, pc_send, pc_recv,
):
    me = lax.axis_index("shard")
    rep = lax.axis_index("rep")
    core = lax.rem(rep, 2)
    z = rep // 2
    sibling = (me, rep + 1 - 2 * core)
    speers = [(lax.rem(me + d, n), rep) for d in range(1, n)]
    zs = [lax.rem(z + d, nz) for d in range(nz)]
    zpeers = [(me, zs[d] * 2 + core) for d in range(1, nz)]
    barrier([sibling] + speers + zpeers)
    half = pg.shape[1] // 2
    piece = half // PIECES
    chunk = piece // nz

    order = [1, 3, 2, 0] if n == 4 else list(range(1, n)) + [0]
    sent = []

    def go(*args):
        cp = remote(*args)
        cp.start()
        sent.append(cp)
        return cp

    def spot(side, c, off, size):
        return pl.ds(pl.multiple_of(side * half + c * piece + off, 16), size)

    firsts, seconds, thirds, fourths, fifths = {}, {}, {}, {}, []
    for c in range(PIECES):
        for d in order:
            s = lax.rem(me + d, n)
            firsts[c, d] = go(
                pg.at[s, spot(1 - core, c, 0, piece)], sib_buf.at[c, s],
                a_send.at[c, d], a_recv.at[c, d], sibling,
            )
    pz = [
        go(pay, pays.at[core, me, z], pz_send.at[d], pz_recv.at[d], zpeers[d - 1])
        for d in range(1, nz)
    ]
    pays[core, me, z] = pay[...]

    def pair(c):
        for d in order:
            s = lax.rem(me + d, n)
            firsts[c, d].wait_recv()
            both = pg[s, spot(core, c, 0, piece), :].astype(F32) + sib_buf[c, s].astype(F32)
            chip[c, s] = both.astype(BF16)
            if d:
                seconds[c, d] = go(
                    chip.at[c, s], grp_buf.at[c, me], b_send.at[c, d], b_recv.at[c, d], speers[d - 1]
                )

    def group(c):
        total = chip[c, me].astype(F32)
        for d in range(1, n):
            seconds[c, d].wait_recv()
            total = total + grp_buf[c, lax.rem(me - d + n, n)].astype(F32)
        mine[c] = total.astype(BF16)
        for d in range(1, nz):
            part = pl.ds(pl.multiple_of(zs[d] * chunk, 16), chunk)
            thirds[c, d] = go(
                mine.at[c, part], z_buf.at[c, z], c_send.at[c, d], c_recv.at[c, d], zpeers[d - 1]
            )

    def column(c):
        total = mine[c, pl.ds(pl.multiple_of(z * chunk, 16), chunk), :].astype(F32)
        for d in range(1, nz):
            thirds[c, d].wait_recv()
            total = total + z_buf[c, lax.rem(z - d + nz, nz)].astype(F32)
        at = spot(core, c, z * chunk, chunk)
        out[at, :] = total.astype(BF16)
        for d in range(1, nz):
            fourths[c, d] = go(
                out.at[at], out.at[at], d_send.at[c, d], d_recv.at[c, d], zpeers[d - 1]
            )
        fifths.append(go(out.at[at], out.at[at], e_send.at[c, 0], e_recv.at[c, 0], sibling))

    def share(c):
        for d in range(1, nz):
            fourths[c, d].wait_recv()
            at = spot(core, c, lax.rem(z - d + nz, nz) * chunk, chunk)
            fifths.append(go(out.at[at], out.at[at], e_send.at[c, d], e_recv.at[c, d], sibling))

    for c in range(PIECES):
        pair(c)
    for cp in pz:
        cp.wait_recv()
    group(0)
    ps = [
        go(pays.at[core, me], pays.at[core, me], ps_send.at[d], ps_recv.at[d], speers[d - 1])
        for d in range(1, n)
    ]
    for c in range(1, PIECES):
        group(c)
        column(c - 1)
    for cp in ps:
        cp.wait_recv()
    pc = go(pays.at[core], pays.at[core], pc_send, pc_recv, sibling)
    column(PIECES - 1)
    for c in range(PIECES):
        share(c)
    for cp in fifths:
        cp.wait_recv()
    pc.wait_recv()
    for cp in sent:
        cp.wait_send()


def reduce_grads(n, nz, pg, pay):
    vmem = pl.BlockSpec(memory_space=pltpu.VMEM)
    dma = pltpu.SemaphoreType.DMA
    rows, width = pg.shape[1:]
    piece = rows // 2 // PIECES
    return pl.pallas_call(
        functools.partial(reduce_kernel, n, nz),
        out_shape=[
            jax.ShapeDtypeStruct((rows, width), BF16),
            jax.ShapeDtypeStruct((2, n, nz) + pay.shape, BF16),
        ],
        in_specs=[vmem] * 2,
        out_specs=[vmem] * 2,
        scratch_shapes=[
            pltpu.VMEM((PIECES, n, piece, width), BF16),
            pltpu.VMEM((PIECES, n, piece, width), BF16),
            pltpu.VMEM((PIECES, n, piece, width), BF16),
            pltpu.VMEM((PIECES, piece, width), BF16),
            pltpu.VMEM((PIECES, nz, piece // nz, width), BF16),
            dma((PIECES, n)), dma((PIECES, n)), dma((PIECES, n)), dma((PIECES, n)),
            dma((PIECES, nz)), dma((PIECES, nz)), dma((PIECES, nz)),
            dma((PIECES, nz)), dma((PIECES, nz)), dma((PIECES, nz)),
            dma((nz,)), dma((nz,)), dma((n,)), dma((n,)), dma, dma,
        ],
        compiler_params=pltpu.CompilerParams(
            collective_id=1, has_side_effects=True, vmem_limit_bytes=58 * MIB
        ),
        name="reduce_grads",
    )(pg, pay)


def prep_kernel(
    n, steps, labels, time_table, class_table, b_ada, b_qv, b_out, b_up, b_down,
    cond_ref, silu_ref, blocks_ref, bada_ref, bias_ref, rows, sems,
):
    me = lax.axis_index("shard")
    batch, width = cond_ref.shape
    copies = []
    for i in range(batch):
        for k, (table, index) in enumerate(((time_table, steps), (class_table, labels))):
            cp = pltpu.make_async_copy(
                table.at[pl.ds(index[i], 1)], rows.at[k, i], sems.at[k, i]
            )
            cp.start()
            copies.append(cp)

    def placed(value, s, total):
        size = value.shape[1]
        parts = [value.astype(F32)]
        if s:
            parts = [jnp.zeros((1, s * size), F32)] + parts
        if (s + 1) * size < total:
            parts = parts + [jnp.zeros((1, total - (s + 1) * size), F32)]
        return jnp.concatenate(parts, axis=1) if len(parts) > 1 else parts[0]

    for s in range(n):
        @pl.when(me == s)
        def _(s=s):
            bada_ref[...] = placed(b_ada[...], s, 6 * width)
            qv = placed(b_qv[...], s, 2 * width)
            up = placed(b_up[...], s, 4 * width)
            bias_ref[0:1, :] = qv[:, :width]
            bias_ref[1:2, :] = qv[:, width:]
            bias_ref[2:3, :] = placed(b_out[...], s, width)
            for j in range(4):
                bias_ref[3 + j : 4 + j, :] = up[:, j * width : (j + 1) * width]
            bias_ref[7:8, :] = placed(b_down[...], s, width)

    for cp in copies:
        cp.wait()
    cond = jnp.concatenate([rows[0, i] + rows[1, i] for i in range(batch)])
    cond_ref[...] = cond
    silu = cond * jax.nn.sigmoid(cond)
    silu_ref[...] = silu
    share = width // n
    padded = jnp.concatenate([silu, jnp.zeros((16 - batch, width), F32)])
    for p in range(n):
        blocks_ref[p] = padded[:, p * share : (p + 1) * share].astype(BF16)


def prepare(n, timesteps, labels, time_table, class_table, biases):
    batch, width = timesteps.shape[0], time_table.shape[1]
    vmem = pl.BlockSpec(memory_space=pltpu.VMEM)
    hbm = pl.BlockSpec(memory_space=pl.ANY)
    smem = pl.BlockSpec(memory_space=pltpu.SMEM)
    return pl.pallas_call(
        functools.partial(prep_kernel, n),
        out_shape=[
            jax.ShapeDtypeStruct((batch, width), F32),
            jax.ShapeDtypeStruct((batch, width), F32),
            jax.ShapeDtypeStruct((n, 16, width // n), BF16),
            jax.ShapeDtypeStruct((1, 6 * width), F32),
            jax.ShapeDtypeStruct((8, width), F32),
        ],
        in_specs=[smem] * 2 + [hbm] * 2 + [vmem] * 5,
        out_specs=[vmem] * 5,
        scratch_shapes=[
            pltpu.VMEM((2, batch, 1, width), F32),
            pltpu.SemaphoreType.DMA((2, batch)),
        ],
        compiler_params=pltpu.CompilerParams(vmem_limit_bytes=58 * MIB),
        name="prepare",
    )(timesteps, labels, time_table, class_table, *[b[None, :] for b in biases])


def finish_kernel(
    n, batch, own, pays, w_ada, dmod, cond_ref,
    cond_grad, g_ada, gb_ada, g_qkv, gb_qv, g_out, gb_out, g_up, gb_up, g_down, gb_down, wide,
):
    me = lax.axis_index("shard")
    for t in range(3):
        g_qkv[:, t * D : (t + 1) * D] = own[t * 96 : (t + 1) * 96, :].astype(F32)
    g_out[...] = own[288:384, :].astype(F32)
    for t in range(4):
        g_up[:, t * D : (t + 1) * D] = own[(4 + t) * 96 : (5 + t) * 96, :].astype(F32)
    g_down[...] = own[768:, :].astype(F32)

    share = D // n
    rows_of = pl.ds(pl.multiple_of(me * share, 8), share)
    silu = jnp.concatenate([pays[6 * batch + i] for i in range(batch)])
    sums = []
    for j in range(6):
        dm = jnp.concatenate([pays[6 * i + j] for i in range(batch)])
        wide[...] = mm_at(silu, dm)
        g_ada[:, j * D : (j + 1) * D] = wide[rows_of, :]
        sums.append(cols(dm.astype(F32)))
    ada = jnp.concatenate(sums, axis=1)
    gb = [cols(pays[7 * batch + i].astype(F32)) for i in range(8)]
    qv = jnp.concatenate(gb[0:2], axis=1)
    for s in range(n):
        @pl.when(me == s)
        def _(s=s):
            def part(value):
                size = value.shape[1] // n
                return value[:, s * size : (s + 1) * size]

            gb_ada[...] = part(ada)
            gb_qv[...] = part(qv)
            gb_out[...] = part(gb[2])
            gb_up[...] = part(jnp.concatenate(gb[3:7], axis=1))
            gb_down[...] = part(gb[7])

    total = jnp.zeros((3 * batch, D), F32)
    for j in range(6):
        dm = jnp.concatenate([dmod[i, j : j + 1, :] for i in range(batch)])
        high = dm.astype(BF16).astype(F32)
        middle = (dm - high).astype(BF16).astype(F32)
        low = dm - high - middle
        three = jnp.concatenate([high, middle, low]).astype(BF16)
        total = total + mm_bt(three, w_ada[:, j * D : (j + 1) * D])
    cond = cond_ref[...]
    sig = jax.nn.sigmoid(cond)
    grad = total[:batch] + total[batch : 2 * batch] + total[2 * batch :]
    cond_grad[...] = grad * (sig * (1.0 + cond * (1.0 - sig)))


def finish(n, own, pays, w_ada, dmod, cond):
    batch = cond.shape[0]
    vmem = pl.BlockSpec(memory_space=pltpu.VMEM)
    shapes = [(batch, D), (D // n, 6 * D), (1, 6 * D // n), (D // n, 3 * D), (1, 2 * D // n), (D // n, D)]
    shapes += [(1, D // n), (D // n, 4 * D), (1, 4 * D // n), (4 * D // n, D), (1, D // n)]
    return pl.pallas_call(
        functools.partial(finish_kernel, n, batch),
        out_shape=[jax.ShapeDtypeStruct(shape, F32) for shape in shapes],
        in_specs=[vmem] * 5,
        out_specs=[vmem] * 11,
        scratch_shapes=[pltpu.VMEM((D, D), F32)],
        compiler_params=pltpu.CompilerParams(vmem_limit_bytes=58 * MIB),
        name="finish",
    )(own, pays, w_ada, dmod, cond)


def body(
    n, reps,
    latents, cotangent, timesteps, labels, time_table, class_table,
    w_ada, b_ada, w_qkv, b_qv, w_out, b_out, w_up, b_up, w_down, b_down,
):
    batch, length, width = latents.shape
    cond, silu, blocks, bada, bias = prepare(
        n, timesteps, labels, time_table, class_table, (b_ada, b_qv, b_out, b_up, b_down)
    )
    wqkv, wout, wup, wdown, modul, bias = gather_weights(
        n, w_qkv, w_out, w_up, w_down, w_ada, blocks, bada, bias
    )
    w_late, _ = lax.optimization_barrier((w_ada, modul))
    w_ada_full = lax.all_gather(w_late, "shard", axis=0, tiled=True)
    block_out, input_grad, dmod, pg, pay = run_block(
        latents, cotangent, modul[:batch].reshape(batch, 6, width), bias, silu, wqkv, wout, wup, wdown
    )
    nz = reps // 2
    if reps % 2 == 0 and pg.shape[1] % (32 * PIECES * nz) == 0:
        own, pays = reduce_grads(n, nz, pg, pay)
    else:
        own = lax.psum(lax.psum_scatter(pg.astype(F32), "shard", scatter_dimension=0), "rep")
        pays = lax.all_gather(pay, ("shard", "rep"))
    pays = pays.reshape((-1,) + pay.shape).transpose(1, 0, 2)
    cond_grad, *grads = finish(n, own, pays, w_ada_full, dmod, cond)
    return (block_out, input_grad, cond_grad) + tuple(
        g.reshape(-1) if i % 2 else g for i, g in enumerate(grads)
    )


def solution(mesh):
    both = ("shard", "rep")
    placed = (P(both, None, None), P(both, None, None), P(both), P(both), P(), P()) + (
        P("shard", None),
        P("shard"),
    ) * 5
    return jax.shard_map(
        functools.partial(body, mesh.shape["shard"], mesh.shape["rep"]),
        mesh=mesh,
        in_specs=placed,
        out_specs=(P(both, None, None), P(both, None, None), P(both, None))
        + (P("shard", None), P("shard")) * 5,
        check_vma=False,
    )
```

```python
import functools
import math

import jax
import jax.numpy as jnp
from jax import lax
from jax.experimental import pallas as pl
from jax.experimental.pallas import tpu as pltpu
from jax.sharding import PartitionSpec as P

H = 6
HD = 64
D = 384
TILES = 12
PIECES = 3
EPS = 1e-06
GELU_C = 0.7978845608028654
MESH = pl.DeviceIdType.MESH
F32 = jnp.float32
BF16 = jnp.bfloat16
MIB = 1024 * 1024


def mm(a, b):
    return lax.dot_general(a, b, (((1,), (0,)), ((), ())), preferred_element_type=F32)


def mm_bt(a, b):
    return lax.dot_general(a, b, (((1,), (1,)), ((), ())), preferred_element_type=F32)


def mm_at(a, b):
    return lax.dot_general(a, b, (((0,), (0,)), ((), ())), preferred_element_type=F32)


def row(vals):
    return jnp.mean(vals, axis=-1, keepdims=True)


def cols(vals):
    return jnp.sum(vals, axis=0, keepdims=True)


def barrier(peers):
    sem = pltpu.get_barrier_semaphore()
    for peer in peers:
        pl.semaphore_signal(sem, inc=1, device_id=peer, device_id_type=MESH)
    pl.semaphore_wait(sem, len(peers))


def remote(src, dst, send, recv, peer):
    return pltpu.make_async_remote_copy(
        src_ref=src, dst_ref=dst, send_sem=send, recv_sem=recv, device_id=peer, device_id_type=MESH
    )


def gather_kernel(
    n, w0, w1, w2, w3, wada, silu, bada, bias,
    o0, o1, o2, o3, omod, obias,
    silu_buf, mod_send, mod_buf, bias_buf, l_sem,
    g_send, g_recv, f_send, f_recv, s_send, s_recv, m_send, m_recv, b_send, b_recv,
):
    me = lax.axis_index("shard")
    rep = lax.axis_index("rep")
    core = lax.rem(rep, 2)
    sibling = (me, rep + 1 - 2 * core)
    peers = [(lax.rem(me + d, n), rep) for d in range(1, n)]
    barrier(peers + [sibling])

    small = []
    for d in range(1, n):
        peer = peers[d - 1]
        cp = remote(silu.at[peer[0]], silu_buf.at[me], s_send.at[d], s_recv.at[d], peer)
        cp.start()
        bp = remote(bias, bias_buf.at[me], b_send.at[d], b_recv.at[d], peer)
        bp.start()
        small.append((cp, bp))

    mats = [(w0, o0), (w1, o1), (w2, o2), (w3, o3)]
    across = me + 1 - 2 * lax.rem(me, 2)
    along = me + 2 - 4 * (me // 2)
    first = across * (1 - core) + along * core
    second = across * core + along * (1 - core)

    def block(w, origin):
        rows = w.shape[0]
        return pl.ds(pl.multiple_of(origin * rows + core * (rows // 2), 16), rows // 2)

    pushes = {}
    for m, (w, o) in enumerate(mats):
        half = w.shape[0] // 2
        mine = w.at[pl.ds(pl.multiple_of(core * half, 16), half)]
        for k, peer in enumerate((first, second)):
            cp = remote(
                mine, o.at[block(w, me)], g_send.at[m, k], g_recv.at[m, k], (peer, rep)
            )
            cp.start()
            pushes[m, k] = cp
    locals_ = []
    for m, (w, o) in enumerate(mats):
        rows = w.shape[0]
        cp = pltpu.make_async_copy(w, o.at[pl.ds(pl.multiple_of(me * rows, 16), rows)], l_sem.at[m])
        cp.start()
        locals_.append(cp)

    def relay(m):
        w, o = mats[m]
        pushes[m, 0].wait_recv()
        at = block(w, first)
        cp = remote(o.at[at], o.at[at], g_send.at[m, 2], g_recv.at[m, 2], (second, rep))
        cp.start()
        pushes[m, 2] = cp
        cp = remote(o.at[at], o.at[at], f_send.at[m, 0], f_recv.at[m, 0], sibling)
        cp.start()
        passed.append(cp)

    passed = []
    silu_buf[me] = silu[me]
    for cp, _ in small:
        cp.wait_recv()
    part = mm(silu_buf[...].reshape(n * 16, silu.shape[2]), wada[...])
    bada_v = bada[...]
    for p in range(n):
        mod_send[p] = part[p * 16 : p * 16 + 8] + bada_v
    mods = []
    relay(0)
    relay(1)
    for d in range(1, n):
        peer = peers[d - 1]
        cp = remote(mod_send.at[peer[0]], mod_buf.at[me], m_send.at[d], m_recv.at[d], peer)
        cp.start()
        mods.append(cp)
    mod_buf[me] = mod_send[me]
    relay(2)
    relay(3)
    bias_buf[me] = bias[...]
    for _, bp in small:
        bp.wait_recv()
    total = bias_buf[0]
    for p in range(1, n):
        total = total + bias_buf[p]
    obias[...] = total
    for cp in mods:
        cp.wait_recv()
    total = mod_buf[0]
    for p in range(1, n):
        total = total + mod_buf[p]
    omod[...] = total


    def hand(m, k, origin):
        w, o = mats[m]
        pushes[m, k].wait_recv()
        at = block(w, origin)
        cp = remote(o.at[at], o.at[at], f_send.at[m, k], f_recv.at[m, k], sibling)
        cp.start()
        passed.append(cp)

    for m in range(4):
        hand(m, 1, second)
    for m in range(4):
        hand(m, 2, 3 - me)
    for cp in passed + locals_:
        cp.wait()
    for cp in pushes.values():
        cp.wait_send()
    for cp, bp in small:
        cp.wait_send()
        bp.wait_send()
    for cp in mods:
        cp.wait_send()


def gather_weights(n, w_qkv, w_out, w_up, w_down, w_ada, silu, bada, bias):
    mats = (w_qkv, w_out, w_up, w_down)
    vmem = pl.BlockSpec(memory_space=pltpu.VMEM)
    hbm = pl.BlockSpec(memory_space=pl.ANY)
    dma = pltpu.SemaphoreType.DMA
    return pl.pallas_call(
        functools.partial(gather_kernel, n),
        out_shape=[jax.ShapeDtypeStruct((n * w.shape[0], w.shape[1]), BF16) for w in mats]
        + [jax.ShapeDtypeStruct((8, bada.shape[1]), F32), jax.ShapeDtypeStruct(bias.shape, F32)],
        in_specs=[hbm] * 4 + [vmem] * 4,
        out_specs=[hbm] * 4 + [vmem] * 2,
        scratch_shapes=[
            pltpu.VMEM(silu.shape, BF16),
            pltpu.VMEM((n, 8, bada.shape[1]), F32),
            pltpu.VMEM((n, 8, bada.shape[1]), F32),
            pltpu.VMEM((n,) + bias.shape, F32),
            dma((4,)), dma((4, n)), dma((4, n)), dma((4, n)), dma((4, n)),
            dma((n,)), dma((n,)), dma((n,)), dma((n,)), dma((n,)), dma((n,)),
        ],
        compiler_params=pltpu.CompilerParams(
            collective_id=0, has_side_effects=True, vmem_limit_bytes=58 * MIB
        ),
        name="gather_weights",
    )(*mats, w_ada, silu, bada, bias)


def block_kernel(
    lat_ref, cot_ref, mod_ref, bias_ref, silu_ref, wqkv, wout, wup, wdown,
    out_ref, ing_ref, dmod_ref, pg_ref, pay_ref,
    gb_ref, dm_s, acc, proj_s, prob_s, heads_s, act_s, slope_s, dproj_s,
):
    step = pl.program_id(0)
    last = pl.num_programs(0) - 1

    @pl.when(step == 0)
    def _():
        acc[...] = jnp.zeros_like(acc)
        gb_ref[...] = jnp.zeros_like(gb_ref)

    mod = mod_ref[0]
    shift1, scale1, gate1, shift2, scale2, gate2 = [mod[i : i + 1] for i in range(6)]
    bias = bias_ref[...]
    lat = lat_ref[0].astype(F32)
    centred = lat - row(lat)
    recip1 = lax.rsqrt(row(centred * centred) + EPS)
    normed1 = centred * recip1
    attn_in = (normed1 * (1.0 + scale1) + shift1).astype(BF16)
    for j in range(3):
        part = mm(attn_in, wqkv[:, j * D : (j + 1) * D])
        if j == 0:
            part = part + bias[0:1]
        if j == 2:
            part = part + bias[1:2]
        proj_s[:, j * D : (j + 1) * D] = part.astype(BF16)

    low = lax.broadcasted_iota(jnp.int32, (256, 128), 1) < HD
    zero = jnp.zeros((256, 128), BF16)
    scale = 1.0 / math.sqrt(HD)
    for pair in range(H // 2):
        at = pair * 128
        q = proj_s[:, at : at + 128]
        k = proj_s[:, D + at : D + at + 128]
        v = proj_s[:, 2 * D + at : 2 * D + at + 128]
        outs = []
        for side in range(2):
            qm = jnp.where(low, q, zero) if side == 0 else jnp.where(low, zero, q)
            s = mm_bt(qm, k) * scale
            e = jnp.exp(s - jnp.max(s, axis=-1, keepdims=True))
            p = e * (1.0 / jnp.sum(e, axis=-1, keepdims=True))
            prob_s[2 * pair + side] = p
            outs.append(mm(p.astype(BF16), v))
        heads_s[:, at : at + 128] = jnp.where(low, outs[0], outs[1]).astype(BF16)

    attended = mm(heads_s[...], wout[...]) + bias[2:3]
    mid = lat + gate1 * attended
    centred = mid - row(mid)
    recip2 = lax.rsqrt(row(centred * centred) + EPS)
    normed2 = centred * recip2
    mlp_in = (normed2 * (1.0 + scale2) + shift2).astype(BF16)
    down = jnp.zeros((256, D), F32)
    for j in range(4):
        at = slice(j * D, (j + 1) * D)
        u = mm(mlp_in, wup[:, at]) + bias[3 + j : 4 + j]
        sq = u * u
        t = jnp.tanh(GELU_C * u * (1.0 + 0.044715 * sq))
        half = 0.5 * (1.0 + t)
        act = (u * half).astype(BF16)
        act_s[:, at] = act
        slope_s[:, at] = half + 0.5 * u * (1.0 - t * t) * (GELU_C + 3.0 * 0.044715 * GELU_C * sq)
        down = down + mm(act, wdown[at, :])
    down = down + bias[7:8]
    out_ref[0] = mid + gate2 * down

    dout = cot_ref[0].astype(F32)
    dmod_ref[0, 5:6, :] = cols(dout * down)
    dmlp = (dout * gate2).astype(BF16)
    gb_ref[7:8, :] += cols(dmlp.astype(F32))
    dmlp_in = jnp.zeros((256, D), F32)
    for j in range(4):
        at = slice(j * D, (j + 1) * D)
        acc[8 + j] += mm_at(act_s[:, at], dmlp)
        dup = (mm_bt(dmlp, wdown[at, :]) * slope_s[:, at]).astype(BF16)
        gb_ref[3 + j : 4 + j, :] += cols(dup.astype(F32))
        acc[4 + j] += mm_at(mlp_in, dup)
        dmlp_in = dmlp_in + mm_bt(dup, wup[:, at])
    dmod_ref[0, 4:5, :] = cols(dmlp_in * normed2)
    dmod_ref[0, 3:4, :] = cols(dmlp_in)
    g2 = dmlp_in * (1.0 + scale2)
    dmid = dout + recip2 * (g2 - row(g2) - normed2 * row(g2 * normed2))
    dmod_ref[0, 2:3, :] = cols(dmid * attended)
    dattn = (dmid * gate1).astype(BF16)
    gb_ref[2:3, :] += cols(dattn.astype(F32))
    acc[3] += mm_at(heads_s[...], dattn)
    dheads = mm_bt(dattn, wout[...]).astype(BF16)
    for pair in range(H // 2):
        at = pair * 128
        q = proj_s[:, at : at + 128]
        k = proj_s[:, D + at : D + at + 128]
        v = proj_s[:, 2 * D + at : 2 * D + at + 128]
        dh = dheads[:, at : at + 128]
        dqs, dks, dvs = [], [], []
        for side in range(2):
            p = prob_s[2 * pair + side]
            dhm = jnp.where(low, dh, zero) if side == 0 else jnp.where(low, zero, dh)
            dvs.append(mm_at(p.astype(BF16), dh))
            dp = mm_bt(dhm, v)
            delta = jnp.sum(p * dp, axis=-1, keepdims=True)
            ds = (p * (dp - delta)).astype(BF16)
            dqs.append(mm(ds, k))
            dks.append(mm_at(ds, q))
        dproj_s[:, at : at + 128] = (jnp.where(low, dqs[0], dqs[1]) * scale).astype(BF16)
        dproj_s[:, D + at : D + at + 128] = (jnp.where(low, dks[0], dks[1]) * scale).astype(BF16)
        dproj_s[:, 2 * D + at : 2 * D + at + 128] = jnp.where(low, dvs[0], dvs[1]).astype(BF16)
    dattn_in = jnp.zeros((256, D), F32)
    for j in range(3):
        at = slice(j * D, (j + 1) * D)
        dpj = dproj_s[:, at]
        acc[j] += mm_at(attn_in, dpj)
        dattn_in = dattn_in + mm_bt(dpj, wqkv[:, at])
        if j != 1:
            gb_ref[j // 2 : j // 2 + 1, :] += cols(dpj.astype(F32))
    dmod_ref[0, 1:2, :] = cols(dattn_in * normed1)
    dmod_ref[0, 0:1, :] = cols(dattn_in)
    g1 = dattn_in * (1.0 + scale1)
    ing_ref[0] = dmid + recip1 * (g1 - row(g1) - normed1 * row(g1 * normed1))

    for j in range(6):
        dm_s[pl.ds(step * 6 + j, 1), :] = dmod_ref[0, j : j + 1, :]

    @pl.when(step == last)
    def _():
        batch = silu_ref.shape[0]
        fill = pay_ref.shape[0] - 7 * batch - 8
        pay_ref[...] = jnp.concatenate(
            [dm_s[...], silu_ref[...], gb_ref[...], jnp.zeros((fill, D), F32)]
        ).astype(BF16)
        for s in range(4):
            for t in range(8):
                pg_ref[s, t * 96 : (t + 1) * 96, :] = acc[t, s * 96 : (s + 1) * 96, :].astype(BF16)
            pg_ref[s, 768:1152, :] = acc[8 + s].astype(BF16)


def run_block(latents, cotangent, modul, bias, silu, wqkv, wout, wup, wdown):
    batch, length, width = latents.shape
    tok = pl.BlockSpec((1, length, width), lambda i: (i, 0, 0))
    mod = pl.BlockSpec((1, 6, width), lambda i: (i, 0, 0))
    whole = pl.BlockSpec(memory_space=pltpu.VMEM)
    rows = 7 * batch + 8

    def full(a):
        return pl.BlockSpec(a.shape, lambda i: (0, 0))

    return pl.pallas_call(
        block_kernel,
        grid=(batch,),
        in_specs=[tok, tok, mod] + [full(a) for a in (bias, silu, wqkv, wout, wup, wdown)],
        out_specs=[tok, tok, mod, whole, whole],
        out_shape=[
            jax.ShapeDtypeStruct(latents.shape, F32),
            jax.ShapeDtypeStruct(latents.shape, F32),
            jax.ShapeDtypeStruct((batch, 6, width), F32),
            jax.ShapeDtypeStruct((4, 96 * TILES, width), BF16),
            jax.ShapeDtypeStruct((rows + -rows % 16, width), BF16),
        ],
        scratch_shapes=[
            pltpu.VMEM((8, width), F32),
            pltpu.VMEM((6 * batch, width), F32),
            pltpu.VMEM((TILES, D, D), F32),
            pltpu.VMEM((length, 3 * D), BF16),
            pltpu.VMEM((H, length, length), F32),
            pltpu.VMEM((length, D), BF16),
            pltpu.VMEM((length, 4 * D), BF16),
            pltpu.VMEM((length, 4 * D), F32),
            pltpu.VMEM((length, 3 * D), BF16),
        ],
        compiler_params=pltpu.CompilerParams(
            dimension_semantics=("arbitrary",), vmem_limit_bytes=58 * MIB
        ),
        cost_estimate=pl.CostEstimate(flops=9 * 10**9, bytes_accessed=12 * 10**6, transcendentals=2 * 10**6),
        name="block",
    )(latents, cotangent, modul, bias, silu, wqkv, wout, wup, wdown)


def reduce_kernel(
    n, nz, pg, pay, out, pays,
    sib_buf, chip, grp_buf, mine, z_buf,
    a_send, a_recv, b_send, b_recv, c_send, c_recv, d_send, d_recv, e_send, e_recv,
    pz_send, pz_recv, ps_send, ps_recv, pc_send, pc_recv,
):
    me = lax.axis_index("shard")
    rep = lax.axis_index("rep")
    core = lax.rem(rep, 2)
    z = rep // 2
    sibling = (me, rep + 1 - 2 * core)
    speers = [(lax.rem(me + d, n), rep) for d in range(1, n)]
    zs = [lax.rem(z + d, nz) for d in range(nz)]
    zpeers = [(me, zs[d] * 2 + core) for d in range(1, nz)]
    barrier([sibling] + speers + zpeers)
    half = pg.shape[1] // 2
    piece = half // PIECES
    chunk = piece // nz

    order = [1, 3, 2, 0] if n == 4 else list(range(1, n)) + [0]
    sent = []

    def go(*args):
        cp = remote(*args)
        cp.start()
        sent.append(cp)
        return cp

    def spot(side, c, off, size):
        return pl.ds(pl.multiple_of(side * half + c * piece + off, 16), size)

    firsts, seconds, thirds, fourths, fifths = {}, {}, {}, {}, []
    for c in range(PIECES):
        for d in order:
            s = lax.rem(me + d, n)
            firsts[c, d] = go(
                pg.at[s, spot(1 - core, c, 0, piece)], sib_buf.at[c, s],
                a_send.at[c, d], a_recv.at[c, d], sibling,
            )
    pz = [
        go(pay, pays.at[core, me, z], pz_send.at[d], pz_recv.at[d], zpeers[d - 1])
        for d in range(1, nz)
    ]
    pays[core, me, z] = pay[...]

    def pair(c):
        for d in order:
            s = lax.rem(me + d, n)
            firsts[c, d].wait_recv()
            both = pg[s, spot(core, c, 0, piece), :].astype(F32) + sib_buf[c, s].astype(F32)
            chip[c, s] = both.astype(BF16)
            if d:
                seconds[c, d] = go(
                    chip.at[c, s], grp_buf.at[c, me], b_send.at[c, d], b_recv.at[c, d], speers[d - 1]
                )

    def group(c):
        total = chip[c, me].astype(F32)
        for d in range(1, n):
            seconds[c, d].wait_recv()
            total = total + grp_buf[c, lax.rem(me - d + n, n)].astype(F32)
        mine[c] = total.astype(BF16)
        for d in range(1, nz):
            part = pl.ds(pl.multiple_of(zs[d] * chunk, 16), chunk)
            thirds[c, d] = go(
                mine.at[c, part], z_buf.at[c, z], c_send.at[c, d], c_recv.at[c, d], zpeers[d - 1]
            )

    def column(c):
        total = mine[c, pl.ds(pl.multiple_of(z * chunk, 16), chunk), :].astype(F32)
        for d in range(1, nz):
            thirds[c, d].wait_recv()
            total = total + z_buf[c, lax.rem(z - d + nz, nz)].astype(F32)
        at = spot(core, c, z * chunk, chunk)
        out[at, :] = total.astype(BF16)
        for d in range(1, nz):
            fourths[c, d] = go(
                out.at[at], out.at[at], d_send.at[c, d], d_recv.at[c, d], zpeers[d - 1]
            )
        fifths.append(go(out.at[at], out.at[at], e_send.at[c, 0], e_recv.at[c, 0], sibling))

    def share(c):
        for d in range(1, nz):
            fourths[c, d].wait_recv()
            at = spot(core, c, lax.rem(z - d + nz, nz) * chunk, chunk)
            fifths.append(go(out.at[at], out.at[at], e_send.at[c, d], e_recv.at[c, d], sibling))

    for c in range(PIECES):
        pair(c)
    for cp in pz:
        cp.wait_recv()
    group(0)
    ps = [
        go(pays.at[core, me], pays.at[core, me], ps_send.at[d], ps_recv.at[d], speers[d - 1])
        for d in range(1, n)
    ]
    for c in range(1, PIECES):
        group(c)
        column(c - 1)
    for cp in ps:
        cp.wait_recv()
    pc = go(pays.at[core], pays.at[core], pc_send, pc_recv, sibling)
    column(PIECES - 1)
    for c in range(PIECES):
        share(c)
    for cp in fifths:
        cp.wait_recv()
    pc.wait_recv()
    for cp in sent:
        cp.wait_send()


def reduce_grads(n, nz, pg, pay):
    vmem = pl.BlockSpec(memory_space=pltpu.VMEM)
    dma = pltpu.SemaphoreType.DMA
    rows, width = pg.shape[1:]
    piece = rows // 2 // PIECES
    return pl.pallas_call(
        functools.partial(reduce_kernel, n, nz),
        out_shape=[
            jax.ShapeDtypeStruct((rows, width), BF16),
            jax.ShapeDtypeStruct((2, n, nz) + pay.shape, BF16),
        ],
        in_specs=[vmem] * 2,
        out_specs=[vmem] * 2,
        scratch_shapes=[
            pltpu.VMEM((PIECES, n, piece, width), BF16),
            pltpu.VMEM((PIECES, n, piece, width), BF16),
            pltpu.VMEM((PIECES, n, piece, width), BF16),
            pltpu.VMEM((PIECES, piece, width), BF16),
            pltpu.VMEM((PIECES, nz, piece // nz, width), BF16),
            dma((PIECES, n)), dma((PIECES, n)), dma((PIECES, n)), dma((PIECES, n)),
            dma((PIECES, nz)), dma((PIECES, nz)), dma((PIECES, nz)),
            dma((PIECES, nz)), dma((PIECES, nz)), dma((PIECES, nz)),
            dma((nz,)), dma((nz,)), dma((n,)), dma((n,)), dma, dma,
        ],
        compiler_params=pltpu.CompilerParams(
            collective_id=1, has_side_effects=True, vmem_limit_bytes=58 * MIB
        ),
        name="reduce_grads",
    )(pg, pay)


def prep_kernel(
    n, steps, labels, time_table, class_table, b_ada, b_qv, b_out, b_up, b_down,
    cond_ref, silu_ref, blocks_ref, bada_ref, bias_ref, rows, sems,
):
    me = lax.axis_index("shard")
    batch, width = cond_ref.shape
    copies = []
    for i in range(batch):
        for k, (table, index) in enumerate(((time_table, steps), (class_table, labels))):
            cp = pltpu.make_async_copy(
                table.at[pl.ds(index[i], 1)], rows.at[k, i], sems.at[k, i]
            )
            cp.start()
            copies.append(cp)

    def placed(value, s, total):
        size = value.shape[1]
        parts = [value.astype(F32)]
        if s:
            parts = [jnp.zeros((1, s * size), F32)] + parts
        if (s + 1) * size < total:
            parts = parts + [jnp.zeros((1, total - (s + 1) * size), F32)]
        return jnp.concatenate(parts, axis=1) if len(parts) > 1 else parts[0]

    for s in range(n):
        @pl.when(me == s)
        def _(s=s):
            bada_ref[...] = placed(b_ada[...].astype(F32).reshape(1, -1), s, 6 * width)
            qv = placed(b_qv[...].astype(F32).reshape(1, -1), s, 2 * width)
            up = placed(b_up[...].astype(F32).reshape(1, -1), s, 4 * width)
            bias_ref[0:1, :] = qv[:, :width]
            bias_ref[1:2, :] = qv[:, width:]
            bias_ref[2:3, :] = placed(b_out[...].astype(F32).reshape(1, -1), s, width)
            for j in range(4):
                bias_ref[3 + j : 4 + j, :] = up[:, j * width : (j + 1) * width]
            bias_ref[7:8, :] = placed(b_down[...].astype(F32).reshape(1, -1), s, width)

    for cp in copies:
        cp.wait()
    cond = jnp.concatenate([rows[0, i] + rows[1, i] for i in range(batch)])
    cond_ref[...] = cond
    silu = cond * jax.nn.sigmoid(cond)
    silu_ref[...] = silu
    share = width // n
    padded = jnp.concatenate([silu, jnp.zeros((16 - batch, width), F32)])
    for p in range(n):
        blocks_ref[p] = padded[:, p * share : (p + 1) * share].astype(BF16)


def prepare(n, timesteps, labels, time_table, class_table, biases):
    batch, width = timesteps.shape[0], time_table.shape[1]
    vmem = pl.BlockSpec(memory_space=pltpu.VMEM)
    hbm = pl.BlockSpec(memory_space=pl.ANY)
    smem = pl.BlockSpec(memory_space=pltpu.SMEM)
    return pl.pallas_call(
        functools.partial(prep_kernel, n),
        out_shape=[
            jax.ShapeDtypeStruct((batch, width), F32),
            jax.ShapeDtypeStruct((batch, width), F32),
            jax.ShapeDtypeStruct((n, 16, width // n), BF16),
            jax.ShapeDtypeStruct((1, 6 * width), F32),
            jax.ShapeDtypeStruct((8, width), F32),
        ],
        in_specs=[smem] * 2 + [hbm] * 2 + [vmem] * 5,
        out_specs=[vmem] * 5,
        scratch_shapes=[
            pltpu.VMEM((2, batch, 1, width), F32),
            pltpu.SemaphoreType.DMA((2, batch)),
        ],
        compiler_params=pltpu.CompilerParams(vmem_limit_bytes=58 * MIB),
        name="prepare",
    )(timesteps, labels, time_table, class_table, *biases)


def finish_kernel(
    n, batch, own, pays, w_ada, dmod, cond_ref,
    cond_grad, g_ada, gb_ada, g_qkv, gb_qv, g_out, gb_out, g_up, gb_up, g_down, gb_down, wide,
):
    me = lax.axis_index("shard")
    for t in range(3):
        g_qkv[:, t * D : (t + 1) * D] = own[t * 96 : (t + 1) * 96, :].astype(F32)
    g_out[...] = own[288:384, :].astype(F32)
    for t in range(4):
        g_up[:, t * D : (t + 1) * D] = own[(4 + t) * 96 : (5 + t) * 96, :].astype(F32)
    g_down[...] = own[768:, :].astype(F32)

    share = D // n
    rows_of = pl.ds(pl.multiple_of(me * share, 8), share)
    silu = jnp.concatenate([pays[6 * batch + i] for i in range(batch)])
    sums = []
    for j in range(6):
        dm = jnp.concatenate([pays[6 * i + j] for i in range(batch)])
        wide[...] = mm_at(silu, dm)
        g_ada[:, j * D : (j + 1) * D] = wide[rows_of, :]
        sums.append(cols(dm.astype(F32)))
    ada = jnp.concatenate(sums, axis=1)
    gb = [cols(pays[7 * batch + i].astype(F32)) for i in range(8)]
    qv = jnp.concatenate(gb[0:2], axis=1)
    for s in range(n):
        @pl.when(me == s)
        def _(s=s):
            def part(value):
                size = value.shape[1] // n
                return value[:, s * size : (s + 1) * size]

            gb_ada[...] = part(ada)[0]
            gb_qv[...] = part(qv)[0]
            gb_out[...] = part(gb[2])[0]
            gb_up[...] = part(jnp.concatenate(gb[3:7], axis=1))[0]
            gb_down[...] = part(gb[7])[0]

    total = jnp.zeros((3 * batch, D), F32)
    for j in range(6):
        dm = jnp.concatenate([dmod[i, j : j + 1, :] for i in range(batch)])
        high = dm.astype(BF16).astype(F32)
        middle = (dm - high).astype(BF16).astype(F32)
        low = dm - high - middle
        three = jnp.concatenate([high, middle, low]).astype(BF16)
        total = total + mm_bt(three, w_ada[:, j * D : (j + 1) * D])
    cond = cond_ref[...]
    sig = jax.nn.sigmoid(cond)
    grad = total[:batch] + total[batch : 2 * batch] + total[2 * batch :]
    cond_grad[...] = grad * (sig * (1.0 + cond * (1.0 - sig)))


def finish(n, own, pays, w_ada, dmod, cond):
    batch = cond.shape[0]
    vmem = pl.BlockSpec(memory_space=pltpu.VMEM)
    shapes = [(batch, D), (D // n, 6 * D), (6 * D // n,), (D // n, 3 * D), (2 * D // n,), (D // n, D)]
    shapes += [(D // n,), (D // n, 4 * D), (4 * D // n,), (4 * D // n, D), (D // n,)]
    return pl.pallas_call(
        functools.partial(finish_kernel, n, batch),
        out_shape=[jax.ShapeDtypeStruct(shape, F32) for shape in shapes],
        in_specs=[vmem] * 5,
        out_specs=[vmem] * 11,
        scratch_shapes=[pltpu.VMEM((D, D), F32)],
        compiler_params=pltpu.CompilerParams(vmem_limit_bytes=58 * MIB),
        name="finish",
    )(own, pays, w_ada, dmod, cond)


def body(
    n, reps,
    latents, cotangent, timesteps, labels, time_table, class_table,
    w_ada, b_ada, w_qkv, b_qv, w_out, b_out, w_up, b_up, w_down, b_down,
):
    batch, length, width = latents.shape
    cond, silu, blocks, bada, bias = prepare(
        n, timesteps, labels, time_table, class_table, (b_ada, b_qv, b_out, b_up, b_down)
    )
    wqkv, wout, wup, wdown, modul, bias = gather_weights(
        n, w_qkv, w_out, w_up, w_down, w_ada, blocks, bada, bias
    )
    w_late, _ = lax.optimization_barrier((w_ada, modul))
    w_ada_full = lax.all_gather(w_late, "shard", axis=0, tiled=True)
    block_out, input_grad, dmod, pg, pay = run_block(
        latents, cotangent, modul[:batch].reshape(batch, 6, width), bias, silu, wqkv, wout, wup, wdown
    )
    nz = reps // 2
    if reps % 2 == 0 and pg.shape[1] % (32 * PIECES * nz) == 0:
        own, pays = reduce_grads(n, nz, pg, pay)
    else:
        own = lax.psum(lax.psum_scatter(pg.astype(F32), "shard", scatter_dimension=0), "rep")
        pays = lax.all_gather(pay, ("shard", "rep"))
    pays = pays.reshape((-1,) + pay.shape).transpose(1, 0, 2)
    cond_grad, *grads = finish(n, own, pays, w_ada_full, dmod, cond)
    return (block_out, input_grad, cond_grad) + tuple(grads)


def solution(mesh):
    both = ("shard", "rep")
    placed = (P(both, None, None), P(both, None, None), P(both), P(both), P(), P()) + (
        P("shard", None),
        P("shard"),
    ) * 5
    return jax.shard_map(
        functools.partial(body, mesh.shape["shard"], mesh.shape["rep"]),
        mesh=mesh,
        in_specs=placed,
        out_specs=(P(both, None, None), P(both, None, None), P(both, None))
        + (P("shard", None), P("shard")) * 5,
        check_vma=False,
    )
```
